512 devices in a mesh: region: 32 (over x, z), line: 16 (over y, core).
Axes of the slice: x: 4, y: 8, z: 8, core: 2. Of those that a mesh axis runs over, the one named last changes fastest.
Arguments:
- modes_now: float32 [192, 1024, 1024], P('region', 'line'), may hold values from -50 to 50
- modes_prev: float32 [192, 1024, 1024], P('region', 'line'), may hold values from -50 to 50
- extents: int32 [192, 2], replicated, may hold values from 24 to 32, as said below
- partner: int32 [192], replicated, may hold values from 0 to 191, as said below
- offset: int32 [192], replicated, may hold values from -8 to 8
Outputs:
- modes_next: float32 [192, 1024, 1024], P('region', 'line')
The draws below stay inside these ranges and needn't reach their ends.
Inputs may be any that keep to these rules, and one draw needn't show every extreme that they name: `extents`: each row holds the live cells of one rectangle along y, then along z; both are reached by some rectangle in every draw. Every rectangle is the upper partner of exactly one rectangle. Rectangle r is held at region index r // 6; its upper partner is held at the same index or at one next to it (cyclically), and in every draw some partner is held at another index.
All inputs are finite; a program needn't handle non-finite values.
Results may differ from the reference program's by a relative error of at most 0.0003.
Values sent between devices are 32-bit elements; how exact they have to be, the bound alone decides.
No kernel may reach another device: no remote copies, remote signals or barrier semaphores. Data moves between devices by JAX's collectives and lax.ppermute only.
A program may use at most 64 MiB of HBM per device.

```python
import math
import jax
import jax.numpy as jnp
from jax import lax

LX = 1024
SIDE = 32
R_DEV = 6
RECTS = 192


def draw_extents(key, part):
    key = jax.random.fold_in(key, 5)
    key_y, key_z, key_pick = jax.random.split(key, 3)
    lowest = SIDE - SIDE // 4
    along_y = jax.random.randint(key_y, (RECTS,), lowest, SIDE + 1)
    along_z = jax.random.randint(key_z, (RECTS,), lowest, SIDE + 1)
    picks = jax.random.permutation(key_pick, RECTS)
    along_y = along_y.at[picks[0]].set(SIDE).at[picks[1]].set(lowest)
    along_z = along_z.at[picks[1]].set(SIDE).at[picks[0]].set(lowest)
    return jnp.stack([along_y, along_z], axis=1).astype(jnp.int32)


def draw_partner(key, part):
    key = jax.random.fold_in(key, 9)
    key_parity, key_flip, key_slot, key_pair, key_order = jax.random.split(key, 5)
    groups = RECTS // R_DEV
    pair_count = groups // 2
    parity = jax.random.randint(key_parity, (R_DEV, 1), 0, 2)
    flipped = jax.random.randint(key_flip, (R_DEV, pair_count), 0, 2)
    chosen_slot = jax.random.randint(key_slot, (), 0, R_DEV)
    chosen_pair = jax.random.randint(key_pair, (), 0, pair_count)
    slot_ids = jnp.arange(R_DEV)[:, None]
    pair_ids = jnp.arange(pair_count)[None, :]
    flipped = jnp.where((slot_ids == chosen_slot) & (pair_ids == chosen_pair), 1, flipped)
    device = jnp.arange(groups)[None, :]
    shifted = jnp.mod(device - parity, groups)
    pair_of = shifted // 2
    side_of = shifted % 2
    swapped = jnp.take_along_axis(flipped, pair_of, axis=1)
    target = jnp.where(swapped == 1, jnp.mod(device + 1 - 2 * side_of, groups), device)
    orders = jax.vmap(lambda sub_key: jax.random.permutation(sub_key, R_DEV))(jax.random.split(key_order, groups))
    landing = orders[target, slot_ids]
    linked = target * R_DEV + landing
    return linked.T.reshape(RECTS).astype(jnp.int32)


def current_modes(key, part, amplitude, tilt_power):
    base_key = jax.random.fold_in(key, 31)
    key_base, key_tilt = jax.random.split(base_key, 2)
    base = jax.random.truncated_normal(key_base, -6.0, 6.0, (RECTS, SIDE * SIDE, LX), jnp.float32)
    tilt = jax.random.uniform(key_tilt, (RECTS,), jnp.float32, -1.0, 1.0)
    return amplitude * jnp.exp(tilt_power * tilt)[:, None, None] * base


def free_phase(sizes_yz):
    live_y = sizes_yz[:, 0].astype(jnp.float32)[:, None, None]
    live_z = sizes_yz[:, 1].astype(jnp.float32)[:, None, None]
    mode_index = jnp.arange(SIDE * SIDE, dtype=jnp.int32)
    freq_y = (mode_index // SIDE).astype(jnp.float32)[None, :, None] / live_y
    freq_z = (mode_index % SIDE).astype(jnp.float32)[None, :, None] / live_z
    freq_x = jnp.arange(LX, dtype=jnp.float32)[None, None, :] / LX
    return 0.5 * math.pi * jnp.sqrt(freq_x * freq_x + freq_y * freq_y + freq_z * freq_z)


def draw_modes_now(key, part):
    present = current_modes(key, part, 3.0, 0.0)
    return present.astype(jnp.float32)


def draw_modes_prev(key, part):
    present = current_modes(key, part, 3.0, 0.0)
    sizes_yz = draw_extents(key, part)
    key = jax.random.fold_in(key, 23)
    jitter = 0.06 * jax.random.truncated_normal(key, -6.0, 6.0, (RECTS, SIDE * SIDE, LX), jnp.float32)
    phase_angle = free_phase(sizes_yz)
    return (2.0 * jnp.cos(phase_angle) * present - jitter).astype(jnp.float32)


def place_ends(result, stream_key, low, high):
    extent = result.shape
    place = [jax.random.randint(jax.random.fold_in(stream_key, axis), (), 0, extent[axis]) for axis in range(len(extent))]
    result = result.at[tuple(place)].set(low)
    longest = extent.index(max(extent))
    place[longest] = (place[longest] + 1) % extent[longest]
    return result.at[tuple(place)].set(high)


def setup_inputs(seed: int = 0) -> dict:
    key_of = jax.random.split(jax.random.key(seed), 6)
    return {
        "modes_now": draw_modes_now(jax.random.fold_in(key_of[5], 71), 0),
        "modes_prev": draw_modes_prev(jax.random.fold_in(key_of[5], 71), 0),
        "extents": draw_extents(jax.random.fold_in(key_of[5], 71), 0),
        "partner": draw_partner(jax.random.fold_in(key_of[5], 71), 0),
        "offset": place_ends(jax.random.randint(key_of[4], (RECTS,), 0 - SIDE // 4, SIDE // 4 + 1), jax.random.fold_in(key_of[4], 1), 0 - SIDE // 4, (SIDE // 4 + 1) - 1).astype(jnp.int32),
    }


courant = 0.5
coeff_one = 1.5
coeff_two = -0.15
coeff_three = 1.0 / 90.0
highest = lax.Precision.HIGHEST

def cosine_entry(freq, cell, active):
    weight = jnp.where(freq == 0.0, jnp.sqrt(1.0 / active), jnp.sqrt(2.0 / active))
    inside = (freq < active) & (cell < active)
    return jnp.where(inside, weight * jnp.cos(math.pi * freq * (cell + 0.5) / active), 0.0)

def line_table(length):
    grid = jnp.arange(length, dtype=jnp.float32)
    return cosine_entry(grid[:, None], grid[None, :], jnp.float32(length))

def strip_table(sizes_yz, mode_index):
    live_y = sizes_yz[0].astype(jnp.float32)
    live_z = sizes_yz[1].astype(jnp.float32)
    freq_y = (mode_index // SIDE).astype(jnp.float32)
    freq_z = (mode_index % SIDE).astype(jnp.float32)
    unit = jnp.ones_like(live_y)
    row_cells = jnp.stack([0.0 * unit, unit, 2.0 * unit, live_y - 1.0, live_y - 2.0, live_y - 3.0])
    grid = jnp.arange(SIDE, dtype=jnp.float32)
    part_y = cosine_entry(freq_y[:, None], row_cells[None, :], live_y)
    part_z = cosine_entry(freq_z[:, None], grid[None, :], live_z)
    return (part_y[:, :, None] * part_z[:, None, :]).reshape(mode_index.shape[0], 6 * SIDE)

def frequency(sizes_yz, mode_index, length):
    live_y = sizes_yz[0].astype(jnp.float32)
    live_z = sizes_yz[1].astype(jnp.float32)
    freq_y = (mode_index // SIDE).astype(jnp.float32)[:, None] / live_y
    freq_z = (mode_index % SIDE).astype(jnp.float32)[:, None] / live_z
    freq_x = jnp.arange(length, dtype=jnp.float32)[None, :] / length
    phase_angle = courant * math.pi * jnp.sqrt(freq_x * freq_x + freq_y * freq_y + freq_z * freq_z)
    active = (mode_index // SIDE < sizes_yz[0]) & (mode_index % SIDE < sizes_yz[1])
    return (phase_angle, active[:, None])

def shift_matrix(shift_by, live_source, live_target):
    source = jnp.arange(SIDE, dtype=jnp.int32)[:, None]
    target_cells = jnp.arange(SIDE, dtype=jnp.int32)[None, :]
    matches = (source == target_cells - shift_by) & (source < live_source) & (target_cells < live_target)
    return jnp.where(matches, 1.0, 0.0).astype(jnp.float32)

def interface_force(own_rows, upper_rows, lower_rows, mask_up, mask_low):
    upper_diff = [upper_rows[..., level, :] - mask_up * own_rows[..., 3 + level, :] for level in range(3)]
    lower_diff = [lower_rows[..., level, :] - mask_low * own_rows[..., level, :] for level in range(3)]

    def spread_rows(difference):
        return [coeff_one * difference[0] + coeff_two * difference[1] + coeff_three * difference[2], coeff_two * difference[0] + coeff_three * difference[1], coeff_three * difference[0]]
    return jnp.stack(spread_rows(lower_diff) + spread_rows(upper_diff), axis=-2)

def modal_update(current, previous, spectral, phase_angle, active):
    factor = jnp.sinc(phase_angle / (2.0 * math.pi))
    stepped = 2.0 * jnp.cos(phase_angle) * current - previous + courant * courant * factor * factor * spectral
    return jnp.where(active, stepped, 0.0)

def reference(modes_now, modes_prev, extents, partner, offset):
    cosines = line_table(LX)
    all_modes = jnp.arange(SIDE * SIDE, dtype=jnp.int32)
    rect_ids = jnp.arange(RECTS, dtype=jnp.int32)

    def boundary(rect_index):
        strips = strip_table(extents[rect_index], all_modes)
        cell_rows = jnp.dot(modes_now[rect_index], cosines, preferred_element_type=jnp.float32, precision=highest)
        return jnp.dot(cell_rows.T, strips, preferred_element_type=jnp.float32, precision=highest)
    boundary_rows = lax.map(boundary, rect_ids)
    lower_of = jnp.zeros((RECTS,), jnp.int32).at[partner].set(rect_ids)

    def advance(rect_index):
        upper_id = partner[rect_index]
        lower_id = lower_of[rect_index]
        own_rows = boundary_rows[rect_index].reshape(LX, 6, SIDE)
        upper_source = boundary_rows[upper_id].reshape(LX, 6, SIDE)[:, 0:3]
        lower_source = boundary_rows[lower_id].reshape(LX, 6, SIDE)[:, 3:6]
        upper_shift = shift_matrix(offset[rect_index], extents[upper_id, 1], extents[rect_index, 1])
        lower_shift = shift_matrix(-offset[lower_id], extents[lower_id, 1], extents[rect_index, 1])
        upper_rows = jnp.einsum('xez,zw->xew', upper_source, upper_shift, precision=highest)
        lower_rows = jnp.einsum('xez,zw->xew', lower_source, lower_shift, precision=highest)
        forcing = interface_force(own_rows, upper_rows, lower_rows, lax.optimization_barrier(jnp.sum(upper_shift, axis=0)), lax.optimization_barrier(jnp.sum(lower_shift, axis=0)))
        strips = strip_table(extents[rect_index], all_modes)
        mixed = jnp.dot(strips, forcing.reshape(LX, 6 * SIDE).T, preferred_element_type=jnp.float32, precision=highest)
        spectral = jnp.dot(mixed, cosines.T, preferred_element_type=jnp.float32, precision=highest)
        phase_angle, active = frequency(extents[rect_index], all_modes, LX)
        return modal_update(modes_now[rect_index], modes_prev[rect_index], spectral, phase_angle, active)
    return lax.map(advance, rect_ids)
```

```python
import math

import jax
import jax.numpy as jnp
from jax import lax
from jax.experimental import pallas as pl
from jax.experimental.pallas import tpu as pltpu
from jax.sharding import PartitionSpec as P

SIDE = 32
PAIRS = 3
OWN = 6
LANES = 128
A1, A2, A3 = 1.5, -0.15, 1.0 / 90.0
VMEM_LIMIT = 48 * 1024 * 1024

SERIES = [2.0 * (-1.0) ** k / math.factorial(2 * k + 2) for k in range(10)]


def series(u):
    total = jnp.full_like(u, SERIES[-1])
    for coefficient in SERIES[-2::-1]:
        total = total * u + coefficient
    return total


def cosine_entry(freq, cell, live):
    turn = 4.0 * live
    steps = freq * (2.0 * cell + 1.0)
    steps = steps - turn * jnp.floor((steps + 0.5) / turn)
    steps = jnp.minimum(steps, turn - steps)
    flip = steps > live
    steps = jnp.where(flip, 2.0 * live - steps, steps)
    angle = (0.5 * math.pi) * (steps / live)
    u = angle * angle
    value = 1.0 - 0.5 * u * series(u)
    value = jnp.where(flip, -value, value)
    weight = jnp.sqrt(jnp.where(freq == 0.0, 1.0, 2.0) / live)
    return jnp.where((freq < live) & (cell < live), weight * value, 0.0)


def z_table(live_z, to_cells):
    shape = (2 * SIDE, 6 * SIDE)
    row = lax.broadcasted_iota(jnp.int32, shape, 0)
    column = lax.broadcasted_iota(jnp.int32, shape, 1)
    same = (row // SIDE) == ((column // SIDE) % 2)
    row_f = (row % SIDE).astype(jnp.float32)
    column_f = (column % SIDE).astype(jnp.float32)
    freq, cell = (column_f, row_f) if to_cells else (row_f, column_f)
    table = jnp.where(same, cosine_entry(freq, cell, jnp.full(shape, live_z, jnp.float32)), 0.0)
    high = table.astype(jnp.bfloat16).astype(jnp.float32)
    return jnp.where(column < 4 * SIDE, high, table - high).astype(jnp.bfloat16)


def z_apply(table, values):
    high = values.astype(jnp.bfloat16)
    low = (values - high.astype(jnp.float32)).astype(jnp.bfloat16)
    stacked = jnp.concatenate([high, low, high], axis=0)
    return jnp.dot(table, stacked, preferred_element_type=jnp.float32)


def live(extents, rect, which):
    return extents[2 * rect + which].astype(jnp.float32)


def left_half(shape):
    return lax.broadcasted_iota(jnp.int32, shape, len(shape) - 1) < LANES // 2


def encode_kernel(extents, now, out):
    pair = pl.program_id(0)
    first = lax.axis_index("region") * OWN + pair
    left = left_half((2 * SIDE, LANES))
    tables = [z_table(live(extents, first + PAIRS * h, 1), True) for h in range(2)]
    for chunk in range(4):
        lanes = slice(chunk * 256, chunk * 256 + 256)
        one, two = (z_apply(tables[h], now[h, 0, :, lanes]) for h in range(2))
        for part in range(2):
            a = one[:, part * LANES : (part + 1) * LANES]
            b = two[:, part * LANES : (part + 1) * LANES]
            chip = 2 * chunk + part
            out[2 * chip, 0] = jnp.where(left, a, pltpu.roll(b, 64, 1))
            out[2 * chip + 1, 0] = jnp.where(left, pltpu.roll(a, 64, 1), b)


def rows_kernel(extents, modes, rows, tables):
    region = lax.axis_index("region")
    left = left_half((3 * SIDE, LANES))
    index = lax.broadcasted_iota(jnp.int32, (3 * SIDE, LANES), 0)
    freq = (index % SIDE).astype(jnp.float32)
    cell = (index // SIDE).astype(jnp.float32)
    for pair in range(PAIRS):
        first = region * OWN + pair
        live_y = jnp.where(left, live(extents, first, 0), live(extents, first + PAIRS, 0))
        tables[pair] = cosine_entry(freq, cell, live_y)
    for pair in range(PAIRS):
        even, odd = [None] * 3, [None] * 3
        for source in range(16):
            for which, total in ((0, even), (1, odd)):
                block = modes[source, pair, which * SIDE : (which + 1) * SIDE]
                for e in range(3):
                    at = e * SIDE + 2 * source + which
                    term = tables[pair, at : at + 1] * block
                    total[e] = term if total[e] is None else total[e] + term
        for e in range(3):
            rows[pair, e] = even[e] + odd[e]
            rows[pair, 3 + e] = even[e] - odd[e]


def spread(d):
    return [A1 * d[0] + A2 * d[1] + A3 * d[2], A2 * d[0] + A3 * d[1], A3 * d[0]]


def force_kernel(extents, partner, offset, own, up, down, tables, out, near):
    region = lax.axis_index("region")
    count = lax.axis_size("region")
    first = region * OWN
    total = count * OWN
    for pair in range(PAIRS):
        near[pair] = down[pair]
        near[PAIRS + pair] = own[pair]
        near[2 * PAIRS + pair] = up[pair]
    lower_of = [jnp.int32(0)] * OWN
    for w in range(3 * OWN):
        rect = lax.rem(first + total + w - OWN, total)
        target = partner[rect] - first
        for r in range(OWN):
            lower_of[r] = jnp.where(target == r, rect, lower_of[r])
    z = lax.broadcasted_iota(jnp.int32, (SIDE, LANES), 0)
    left = left_half((SIDE, LANES))
    left3 = left_half((3, SIDE, LANES))

    def fetch(rect, row, shift, half):
        place = lax.div(rect, OWN)
        slot = rect - place * OWN
        side = lax.div(slot, PAIRS)
        at = lax.rem(place - region + 1 + count, count) * PAIRS + slot - side * PAIRS
        cells = near[at, row : row + 3]
        cells = pltpu.roll(cells, lax.rem(shift + SIDE, SIDE), 1)
        return jnp.where(side == half, cells, pltpu.roll(cells, LANES // 2, 2))

    for pair in range(PAIRS):
        taken = {}
        for name in ("upper", "lower"):
            pieces, masks = [], []
            for half in range(2):
                r = pair + PAIRS * half
                rect = first + r
                if name == "upper":
                    other = partner[rect]
                    shift = offset[rect]
                    pieces.append(fetch(other, 0, shift, half))
                else:
                    other = lower_of[r]
                    shift = -offset[other]
                    pieces.append(fetch(other, 3, shift, half))
                source = z - shift
                masks.append(
                    jnp.where(
                        (source >= 0)
                        & (source < extents[2 * other + 1])
                        & (z < extents[2 * rect + 1]),
                        1.0,
                        0.0,
                    )
                )
            mask = jnp.where(left, masks[0], masks[1])
            both = jnp.where(left3, pieces[0], pieces[1])
            base = 3 if name == "upper" else 0
            taken[name] = spread([mask * (both[e] - own[pair, base + e]) for e in range(3)])
        even = [taken["lower"][e] + taken["upper"][e] for e in range(3)]
        odd = [taken["lower"][e] - taken["upper"][e] for e in range(3)]
        for source in range(16):
            for which, parts in ((0, even), (1, odd)):
                value = None
                for e in range(3):
                    at = e * SIDE + 2 * source + which
                    term = tables[pair, at : at + 1] * parts[e]
                    value = term if value is None else value + term
                out[source, pair, which * SIDE : (which + 1) * SIDE] = value


def update_kernel(extents, mixed, now, previous, out):
    pair = pl.program_id(0)
    first = lax.axis_index("region") * OWN + pair
    line = lax.axis_index("line")
    left = left_half((2 * SIDE, LANES))
    row = lax.broadcasted_iota(jnp.int32, (2 * SIDE, 256), 0)
    freq_y = (2 * line + row // SIDE).astype(jnp.float32)
    freq_z = (row % SIDE).astype(jnp.float32)
    column = lax.broadcasted_iota(jnp.int32, (1, 256), 1)
    quarter = (0.5 * math.pi) ** 2
    tables, bases, actives = [], [], []
    for h in range(2):
        live_y = live(extents, first + PAIRS * h, 0)
        live_z = live(extents, first + PAIRS * h, 1)
        tables.append(z_table(live_z, False))
        y = freq_y / live_y
        z = freq_z / live_z
        bases.append(quarter * (y * y + z * z))
        actives.append((freq_y < live_y) & (freq_z < live_z))
    for chunk in range(4):
        lanes = slice(chunk * 256, chunk * 256 + 256)
        ones, twos = [], []
        for part in range(2):
            chip = 2 * chunk + part
            a = mixed[2 * chip, 0]
            b = mixed[2 * chip + 1, 0]
            ones.append(jnp.where(left, a, pltpu.roll(b, 64, 1)))
            twos.append(jnp.where(left, pltpu.roll(a, 64, 1), b))
        x = (column + chunk * 256).astype(jnp.float32) * (1.0 / 1024.0)
        along = quarter * (x * x)
        for h, pieces in ((0, ones), (1, twos)):
            spectral = z_apply(tables[h], jnp.concatenate(pieces, axis=1))
            u = bases[h] + along
            s = series(u)
            current = now[h, 0, :, lanes]
            stepped = (2.0 - u * s) * current - previous[h, 0, :, lanes] + 0.25 * s * spectral
            out[h, 0, :, lanes] = jnp.where(actives[h], stepped, 0.0)


def smem():
    return pl.BlockSpec(memory_space=pltpu.SMEM)


def vmem():
    return pl.BlockSpec(memory_space=pltpu.VMEM)


def shards(modes_now, modes_prev, extents, partner, offset):
    f32 = jnp.float32
    extents = extents.reshape(-1)
    now = modes_now.reshape(2, PAIRS, 2 * SIDE, 1024)
    previous = modes_prev.reshape(2, PAIRS, 2 * SIDE, 1024)
    wide = pl.BlockSpec((2, 1, 2 * SIDE, 1024), lambda i: (0, i, 0, 0))
    packed = pl.BlockSpec((16, 1, 2 * SIDE, LANES), lambda i: (0, i, 0, 0))
    packed_shape = jax.ShapeDtypeStruct((16, PAIRS, 2 * SIDE, LANES), f32)
    rows_shape = jax.ShapeDtypeStruct((PAIRS, 6, SIDE, LANES), f32)
    params = pltpu.CompilerParams(vmem_limit_bytes=VMEM_LIMIT)

    with jax.named_scope("encode"):
        sent = pl.pallas_call(
            encode_kernel,
            grid=(PAIRS,),
            out_shape=packed_shape,
            in_specs=[smem(), wide],
            out_specs=packed,
            compiler_params=params,
        )(extents, now)
    held = lax.all_to_all(sent, "line", 0, 0, tiled=True)
    with jax.named_scope("rows"):
        rows, tables = pl.pallas_call(
            rows_kernel,
            out_shape=(rows_shape, jax.ShapeDtypeStruct((PAIRS, 3 * SIDE, LANES), f32)),
            in_specs=[smem(), vmem()],
            out_specs=(vmem(), vmem()),
            compiler_params=params,
        )(extents, held)
    count = lax.axis_size("region")
    up = lax.ppermute(rows, "region", [((i + 1) % count, i) for i in range(count)])
    down = lax.ppermute(rows, "region", [(i, (i + 1) % count) for i in range(count)])
    with jax.named_scope("force"):
        forced = pl.pallas_call(
            force_kernel,
            out_shape=packed_shape,
            in_specs=[smem(), smem(), smem()] + [vmem()] * 4,
            out_specs=vmem(),
            scratch_shapes=[pltpu.VMEM((3 * PAIRS, 6, SIDE, LANES), f32)],
            compiler_params=params,
        )(extents, partner, offset, rows, up, down, tables)
    mixed = lax.all_to_all(forced, "line", 0, 0, tiled=True)
    with jax.named_scope("update"):
        result = pl.pallas_call(
            update_kernel,
            grid=(PAIRS,),
            out_shape=jax.ShapeDtypeStruct(now.shape, f32),
            in_specs=[smem(), packed, wide, wide],
            out_specs=wide,
            compiler_params=params,
        )(extents, mixed, now, previous)
    return result.reshape(modes_now.shape)


def solution(mesh):
    return jax.shard_map(
        shards,
        mesh=mesh,
        in_specs=(P("region", "line", None), P("region", "line", None), P(), P(), P()),
        out_specs=P("region", "line", None),
        check_vma=False,
    )
```

```python
import math

import jax
import jax.numpy as jnp
from jax import lax
from jax.experimental import pallas as pl
from jax.experimental.pallas import tpu as pltpu
from jax.sharding import PartitionSpec as P

SIDE = 32
PAIRS = 3
OWN = 6
LANES = 128
A1, A2, A3 = 1.5, -0.15, 1.0 / 90.0
VMEM_LIMIT = 16 * 1024 * 1024
ENCODE_LIMIT = 63 * 1024 * 1024

SERIES = [2.0 * (-1.0) ** k / math.factorial(2 * k + 2) for k in range(10)]


def series(u, terms):
    total = jnp.full_like(u, SERIES[terms - 1])
    for coefficient in SERIES[: terms - 1][::-1]:
        total = total * u + coefficient
    return total


def cosine_entry(freq, cell, live):
    inverse = 1.0 / live
    turn = 4.0 * live
    steps = freq * (2.0 * cell + 1.0)
    steps = steps - turn * jnp.floor((steps + 0.5) * (0.25 * inverse))
    steps = jnp.minimum(steps, turn - steps)
    flip = steps > live
    steps = jnp.where(flip, 2.0 * live - steps, steps)
    angle = (0.5 * math.pi) * (steps * inverse)
    u = angle * angle
    value = 1.0 - 0.5 * u * series(u, 7)
    value = jnp.where(flip, -value, value)
    weight = jnp.sqrt(jnp.where(freq == 0.0, 1.0, 2.0) * inverse)
    return jnp.where((freq < live) & (cell < live), weight * value, 0.0)


def z_table(live_z, to_cells):
    shape = (SIDE, LANES)
    row = lax.broadcasted_iota(jnp.int32, shape, 0).astype(jnp.float32)
    lane = lax.broadcasted_iota(jnp.int32, shape, 1)
    column = (lane % SIDE).astype(jnp.float32)
    freq, cell = (column, row) if to_cells else (row, column)
    table = cosine_entry(freq, cell, jnp.full(shape, live_z, jnp.float32))
    high = table.astype(jnp.bfloat16).astype(jnp.float32)
    return jnp.where(lane < LANES // 2, high, table - high).astype(jnp.bfloat16)


def z_apply(table, parts):
    values = jnp.concatenate(parts, axis=1)
    high = values.astype(jnp.bfloat16)
    low = (values - high.astype(jnp.float32)).astype(jnp.bfloat16)
    stacked = jnp.concatenate([high, low, high, low], axis=0)
    both = jnp.dot(table, stacked, preferred_element_type=jnp.float32)
    left = left_half((SIDE, LANES))
    return [
        jnp.where(
            left,
            both[:SIDE, i * LANES : (i + 1) * LANES],
            both[SIDE:, i * LANES : (i + 1) * LANES],
        )
        for i in range(len(parts))
    ]


def live(extents, rect, which):
    return extents[which, rect].astype(jnp.float32)


def left_half(shape):
    return lax.broadcasted_iota(jnp.int32, shape, len(shape) - 1) < LANES // 2


def encode_kernel(now, out, held, made, arrived, sent):
    left = left_half((2 * SIDE, LANES))
    inward = [
        pltpu.make_async_copy(now.at[:, i], held.at[i], arrived.at[i]) for i in range(PAIRS)
    ]
    outward = [
        pltpu.make_async_copy(made.at[i], out.at[:, i], sent.at[i]) for i in range(PAIRS)
    ]
    for copy in inward:
        copy.start()
    for pair in range(PAIRS):
        inward[pair].wait()
        for chip in range(8):
            lanes = slice(chip * LANES, chip * LANES + LANES)
            a = held[pair, 0, :, lanes]
            b = held[pair, 1, :, lanes]
            made[pair, 2 * chip] = jnp.where(left, a, pltpu.roll(b, LANES // 2, 1))
            made[pair, 2 * chip + 1] = jnp.where(left, pltpu.roll(a, LANES // 2, 1), b)
        outward[pair].start()
    for copy in outward:
        copy.wait()


def plan_kernel(extents, partner, offset, y_tables, to_cells, to_modes, masks, places):
    region = lax.axis_index("region")
    count = lax.axis_size("region")
    first = region * OWN
    total = count * OWN
    left = left_half((3 * SIDE, LANES))
    index = lax.broadcasted_iota(jnp.int32, (3 * SIDE, LANES), 0)
    freq = (index % SIDE).astype(jnp.float32)
    cell = (index // SIDE).astype(jnp.float32)
    for pair in range(PAIRS):
        one, two = first + pair, first + pair + PAIRS
        live_y = jnp.where(left, live(extents, one, 0), live(extents, two, 0))
        y_tables[pair] = cosine_entry(freq, cell, live_y)
        for h, rect in ((0, one), (1, two)):
            live_z = live(extents, rect, 1)
            to_cells[pair, h * SIDE : (h + 1) * SIDE] = z_table(live_z, True)
            to_modes[pair, h * SIDE : (h + 1) * SIDE] = z_table(live_z, False)
    lower_of = [jnp.int32(0)] * OWN
    for w in range(3 * OWN):
        rect = lax.rem(first + total + w - OWN, total)
        target = partner[rect] - first
        for r in range(OWN):
            lower_of[r] = jnp.where(target == r, rect, lower_of[r])
    z = lax.broadcasted_iota(jnp.int32, (SIDE, LANES), 0)
    left = left_half((SIDE, LANES))
    for pair in range(PAIRS):
        for face in range(2):
            parts = []
            for half in range(2):
                r = pair + PAIRS * half
                rect = first + r
                if face == 1:
                    other = partner[rect]
                    shift = offset[rect]
                else:
                    other = lower_of[r]
                    shift = -offset[other]
                place = lax.div(other, OWN)
                slot = other - place * OWN
                side = lax.div(slot, PAIRS)
                at = 3 * ((pair * 2 + face) * 2 + half)
                places[at] = lax.rem(place - region + 1 + count, count) * PAIRS + slot - side * PAIRS
                places[at + 1] = lax.rem(shift + SIDE, SIDE)
                places[at + 2] = side
                source = z - shift
                inside = (source >= 0) & (source < extents[1, other]) & (z < extents[1, rect])
                parts.append(jnp.where(inside, 1.0, 0.0))
            masks[pair, face] = jnp.where(left, parts[0], parts[1])


def free_kernel(extents, now, previous, base, gain):
    first = lax.axis_index("region") * OWN
    line = lax.axis_index("line")
    row = lax.broadcasted_iota(jnp.int32, (2 * SIDE, 256), 0)
    freq_y = (2 * line + row // SIDE).astype(jnp.float32)
    freq_z = (row % SIDE).astype(jnp.float32)
    column = lax.broadcasted_iota(jnp.int32, (1, 256), 1)
    quarter = (0.5 * math.pi) ** 2
    for r in range(OWN):
        h, pair = r // PAIRS, r % PAIRS
        live_y = live(extents, first + r, 0)
        live_z = live(extents, first + r, 1)
        y = freq_y / live_y
        z = freq_z / live_z
        across = quarter * (y * y + z * z)
        active = (freq_y < live_y) & (freq_z < live_z)
        for chunk in range(4):
            lanes = slice(chunk * 256, chunk * 256 + 256)
            x = (column + chunk * 256).astype(jnp.float32) * (1.0 / 1024.0)
            u = across + quarter * (x * x)
            s = series(u, 9)
            stepped = (2.0 - u * s) * now[h, pair, :, lanes] - previous[h, pair, :, lanes]
            base[h, pair, :, lanes] = jnp.where(active, stepped, 0.0)
            gain[h, pair, :, lanes] = jnp.where(active, 0.25 * s, 0.0)


def rows_kernel(tables, to_cells, modes, rows):
    for pair in range(PAIRS):
        even, odd = [None] * 3, [None] * 3
        for source in range(16):
            for which, total in ((0, even), (1, odd)):
                block = modes[source, pair, which * SIDE : (which + 1) * SIDE]
                for e in range(3):
                    at = e * SIDE + 2 * source + which
                    term = tables[pair, at : at + 1] * block
                    total[e] = term if total[e] is None else total[e] + term
        lower = [even[e] + odd[e] for e in range(3)]
        upper = [even[e] - odd[e] for e in range(3)]
        for i, cells in enumerate(z_apply(to_cells[pair], lower + upper)):
            rows[pair, i] = cells


def spread(d):
    return [A1 * d[0] + A2 * d[1] + A3 * d[2], A2 * d[0] + A3 * d[1], A3 * d[0]]


def force_kernel(places, tables, to_modes, masks, own, up, down, out, near, made, sent):
    copies = []
    for pair in range(PAIRS):
        near[pair] = down[pair]
        near[PAIRS + pair] = own[pair]
        near[2 * PAIRS + pair] = up[pair]
    left = left_half((3, SIDE, LANES))
    for pair in range(PAIRS):
        taken = []
        for face in range(2):
            pieces = []
            for half in range(2):
                at = 3 * ((pair * 2 + face) * 2 + half)
                row = 0 if face == 1 else 3
                cells = near[places[at], row : row + 3]
                cells = pltpu.roll(cells, places[at + 1], 1)
                pieces.append(
                    jnp.where(places[at + 2] == half, cells, pltpu.roll(cells, LANES // 2, 2))
                )
            both = jnp.where(left, pieces[0], pieces[1])
            mask = masks[pair, face]
            taken.append(spread([mask * (both[e] - own[pair, 3 * face + e]) for e in range(3)]))
        even = [taken[0][e] + taken[1][e] for e in range(3)]
        odd = [taken[0][e] - taken[1][e] for e in range(3)]
        sixfold = z_apply(to_modes[pair], even + odd)
        for target in range(16):
            for which, parts in ((0, sixfold[:3]), (1, sixfold[3:])):
                value = None
                for e in range(3):
                    at = e * SIDE + 2 * target + which
                    term = tables[pair, at : at + 1] * parts[e]
                    value = term if value is None else value + term
                made[pair, target, which * SIDE : (which + 1) * SIDE] = value
        copies.append(pltpu.make_async_copy(made.at[pair], out.at[:, pair], sent.at[pair]))
        copies[-1].start()
    for copy in copies:
        copy.wait()


def update_kernel(mixed, base, gain, out, made, sent):
    left = left_half((2 * SIDE, LANES))
    copies = []
    for pair in range(PAIRS):
        for chip in range(8):
            lanes = slice(chip * LANES, chip * LANES + LANES)
            a = mixed[2 * chip, pair]
            b = mixed[2 * chip + 1, pair]
            one = jnp.where(left, a, pltpu.roll(b, LANES // 2, 1))
            two = jnp.where(left, pltpu.roll(a, LANES // 2, 1), b)
            for h, spectral in ((0, one), (1, two)):
                made[pair, h, :, lanes] = base[h, pair, :, lanes] + gain[h, pair, :, lanes] * spectral
        copies.append(pltpu.make_async_copy(made.at[pair], out.at[:, pair], sent.at[pair]))
        copies[-1].start()
    for copy in copies:
        copy.wait()


def smem():
    return pl.BlockSpec(memory_space=pltpu.SMEM)


def vmem():
    return pl.BlockSpec(memory_space=pltpu.VMEM)


def hbm():
    return pl.BlockSpec(memory_space=pltpu.HBM)


def cost(flops, nbytes):
    return pl.CostEstimate(flops=flops, bytes_accessed=nbytes, transcendentals=0)


def shards(modes_now, modes_prev, extents, partner, offset):
    f32 = jnp.float32
    extents = extents.T
    now = modes_now.reshape(2, PAIRS, 2 * SIDE, 1024)
    previous = modes_prev.reshape(2, PAIRS, 2 * SIDE, 1024)
    nbytes = now.size * 4
    wide_shape = jax.ShapeDtypeStruct(now.shape, f32)
    packed_shape = jax.ShapeDtypeStruct((16, PAIRS, 2 * SIDE, LANES), f32)
    rows_shape = jax.ShapeDtypeStruct((PAIRS, 6, SIDE, LANES), f32)
    table_shape = jax.ShapeDtypeStruct((PAIRS, 2 * SIDE, LANES), jnp.bfloat16)
    params = pltpu.CompilerParams(vmem_limit_bytes=VMEM_LIMIT)
    wide_scratch = pltpu.VMEM((PAIRS, 2, 2 * SIDE, 1024), f32)
    packed_scratch = pltpu.VMEM((PAIRS, 16, 2 * SIDE, LANES), f32)
    copied = pltpu.SemaphoreType.DMA((PAIRS,))

    with jax.named_scope("encode"):
        sent = pl.pallas_call(
            encode_kernel,
            out_shape=packed_shape,
            in_specs=[hbm()],
            out_specs=hbm(),
            scratch_shapes=[wide_scratch, packed_scratch, copied, copied],
            compiler_params=pltpu.CompilerParams(vmem_limit_bytes=ENCODE_LIMIT),
            cost_estimate=cost(10**6, 2 * nbytes),
        )(now)
    held = lax.all_to_all(sent, "line", 0, 0, tiled=True)
    with jax.named_scope("plan"):
        y_tables, to_cells, to_modes, masks, places = pl.pallas_call(
            plan_kernel,
            out_shape=(
                jax.ShapeDtypeStruct((PAIRS, 3 * SIDE, LANES), f32),
                table_shape,
                table_shape,
                jax.ShapeDtypeStruct((PAIRS, 2, SIDE, LANES), f32),
                jax.ShapeDtypeStruct((36,), jnp.int32),
            ),
            in_specs=[smem(), smem(), smem()],
            out_specs=(vmem(), vmem(), vmem(), vmem(), smem()),
            compiler_params=params,
            cost_estimate=cost(10**8, 10**6),
        )(extents, partner, offset)
    with jax.named_scope("rows"):
        rows = pl.pallas_call(
            rows_kernel,
            out_shape=rows_shape,
            in_specs=[vmem()] * 3,
            out_specs=vmem(),
            compiler_params=params,
            cost_estimate=cost(10**7, nbytes),
        )(y_tables, to_cells, held)
    count = lax.axis_size("region")
    up = lax.ppermute(rows, "region", [((i + 1) % count, i) for i in range(count)])
    down = lax.ppermute(rows, "region", [(i, (i + 1) % count) for i in range(count)])
    with jax.named_scope("free"):
        base, gain = pl.pallas_call(
            free_kernel,
            out_shape=(wide_shape, wide_shape),
            in_specs=[smem(), vmem(), vmem()],
            out_specs=(vmem(), vmem()),
            compiler_params=params,
            cost_estimate=cost(10**9, 4 * nbytes),
        )(extents, *lax.optimization_barrier((now, previous, rows))[:2])
    up, base, gain = lax.optimization_barrier((up, base, gain))
    with jax.named_scope("force"):
        forced = pl.pallas_call(
            force_kernel,
            out_shape=packed_shape,
            in_specs=[smem()] + [vmem()] * 6,
            out_specs=hbm(),
            scratch_shapes=[pltpu.VMEM((3 * PAIRS, 6, SIDE, LANES), f32), packed_scratch, copied],
            compiler_params=params,
            cost_estimate=cost(10**7, nbytes),
        )(places, y_tables, to_modes, masks, rows, up, down)
    mixed = lax.all_to_all(forced, "line", 0, 0, tiled=True)
    with jax.named_scope("update"):
        result = pl.pallas_call(
            update_kernel,
            out_shape=wide_shape,
            in_specs=[vmem()] * 3,
            out_specs=hbm(),
            scratch_shapes=[wide_scratch, copied],
            compiler_params=params,
            cost_estimate=cost(10**7, 4 * nbytes),
        )(mixed, base, gain)
    return result.reshape(modes_now.shape)


def solution(mesh):
    return jax.shard_map(
        shards,
        mesh=mesh,
        in_specs=(P("region", "line", None), P("region", "line", None), P(), P(), P()),
        out_specs=P("region", "line", None),
        check_vma=False,
    )
```

```python
import math

import jax
import jax.numpy as jnp
from jax import lax
from jax.experimental import pallas as pl
from jax.experimental.pallas import tpu as pltpu
from jax.sharding import PartitionSpec as P

SIDE = 32
PAIRS = 3
OWN = 6
LANES = 128
A1, A2, A3 = 1.5, -0.15, 1.0 / 90.0
VMEM_LIMIT = 16 * 1024 * 1024
ENCODE_LIMIT = 63 * 1024 * 1024
FORCE_LIMIT = 52 * 1024 * 1024

SERIES = [2.0 * (-1.0) ** k / math.factorial(2 * k + 2) for k in range(10)]


def series(u, terms):
    total = jnp.full_like(u, SERIES[terms - 1])
    for coefficient in SERIES[: terms - 1][::-1]:
        total = total * u + coefficient
    return total


def cosine_entry(freq, cell, live):
    inverse = 1.0 / live
    turn = 4.0 * live
    steps = freq * (2.0 * cell + 1.0)
    steps = steps - turn * jnp.floor((steps + 0.5) * (0.25 * inverse))
    steps = jnp.minimum(steps, turn - steps)
    flip = steps > live
    steps = jnp.where(flip, 2.0 * live - steps, steps)
    angle = (0.5 * math.pi) * (steps * inverse)
    u = angle * angle
    value = 1.0 - 0.5 * u * series(u, 7)
    value = jnp.where(flip, -value, value)
    weight = jnp.sqrt(jnp.where(freq == 0.0, 1.0, 2.0) * inverse)
    return jnp.where((freq < live) & (cell < live), weight * value, 0.0)


def z_table(live_z, to_cells):
    shape = (SIDE, LANES)
    row = lax.broadcasted_iota(jnp.int32, shape, 0).astype(jnp.float32)
    lane = lax.broadcasted_iota(jnp.int32, shape, 1)
    column = (lane % SIDE).astype(jnp.float32)
    freq, cell = (column, row) if to_cells else (row, column)
    table = cosine_entry(freq, cell, jnp.full(shape, live_z, jnp.float32))
    high = table.astype(jnp.bfloat16).astype(jnp.float32)
    return jnp.where(lane < LANES // 2, high, table - high).astype(jnp.bfloat16)


def z_apply(table, parts):
    values = jnp.concatenate(parts, axis=1)
    high = values.astype(jnp.bfloat16)
    low = (values - high.astype(jnp.float32)).astype(jnp.bfloat16)
    stacked = jnp.concatenate([high, low, high, low], axis=0)
    both = jnp.dot(table, stacked, preferred_element_type=jnp.float32)
    left = left_half((SIDE, LANES))
    return [
        jnp.where(
            left,
            both[:SIDE, i * LANES : (i + 1) * LANES],
            both[SIDE:, i * LANES : (i + 1) * LANES],
        )
        for i in range(len(parts))
    ]


def live(extents, rect, which):
    return extents[which, rect].astype(jnp.float32)


def left_half(shape):
    return lax.broadcasted_iota(jnp.int32, shape, len(shape) - 1) < LANES // 2


def encode_kernel(now, out, held, made, arrived, sent):
    left = left_half((2 * SIDE, LANES))
    inward, outward = [], []
    for part in range(2 * PAIRS):
        pair, half = part // 2, part % 2
        source = now.at[:, pair, :, pl.ds(half * 512, 512)]
        target = out.at[pl.ds(half * 8, 8), pair]
        inward.append(pltpu.make_async_copy(source, held.at[part], arrived.at[part]))
        outward.append(pltpu.make_async_copy(made.at[part], target, sent.at[part]))
        inward[-1].start()
    for part in range(2 * PAIRS):
        inward[part].wait()
        for chip in range(4):
            lanes = slice(chip * LANES, chip * LANES + LANES)
            a = held[part, 0, :, lanes]
            b = held[part, 1, :, lanes]
            made[part, 2 * chip] = jnp.where(left, a, pltpu.roll(b, LANES // 2, 1))
            made[part, 2 * chip + 1] = jnp.where(left, pltpu.roll(a, LANES // 2, 1), b)
        outward[part].start()
    for copy in outward:
        copy.wait()


def plan_kernel(extents, partner, offset, y_tables, to_cells, to_modes, masks, places):
    region = lax.axis_index("region")
    count = lax.axis_size("region")
    first = region * OWN
    total = count * OWN
    left = left_half((3 * SIDE, LANES))
    index = lax.broadcasted_iota(jnp.int32, (3 * SIDE, LANES), 0)
    freq = (index % SIDE).astype(jnp.float32)
    cell = (index // SIDE).astype(jnp.float32)
    for pair in range(PAIRS):
        one, two = first + pair, first + pair + PAIRS
        live_y = jnp.where(left, live(extents, one, 0), live(extents, two, 0))
        y_tables[pair] = cosine_entry(freq, cell, live_y)
        for h, rect in ((0, one), (1, two)):
            live_z = live(extents, rect, 1)
            to_cells[pair, h * SIDE : (h + 1) * SIDE] = z_table(live_z, True)
            to_modes[pair, h * SIDE : (h + 1) * SIDE] = z_table(live_z, False)
    lower_of = [jnp.int32(0)] * OWN
    for w in range(3 * OWN):
        rect = lax.rem(first + total + w - OWN, total)
        target = partner[rect] - first
        for r in range(OWN):
            lower_of[r] = jnp.where(target == r, rect, lower_of[r])
    z = lax.broadcasted_iota(jnp.int32, (SIDE, LANES), 0)
    left = left_half((SIDE, LANES))
    for pair in range(PAIRS):
        for face in range(2):
            parts = []
            for half in range(2):
                r = pair + PAIRS * half
                rect = first + r
                if face == 1:
                    other = partner[rect]
                    shift = offset[rect]
                else:
                    other = lower_of[r]
                    shift = -offset[other]
                place = lax.div(other, OWN)
                slot = other - place * OWN
                side = lax.div(slot, PAIRS)
                at = 3 * ((pair * 2 + face) * 2 + half)
                places[at] = lax.rem(place - region + 1 + count, count) * PAIRS + slot - side * PAIRS
                places[at + 1] = lax.rem(shift + SIDE, SIDE)
                places[at + 2] = side
                source = z - shift
                inside = (source >= 0) & (source < extents[1, other]) & (z < extents[1, rect])
                parts.append(jnp.where(inside, 1.0, 0.0))
            masks[pair, face] = jnp.where(left, parts[0], parts[1])


def free_kernel(extents, now, previous, both):
    first = lax.axis_index("region") * OWN
    line = lax.axis_index("line")
    row = lax.broadcasted_iota(jnp.int32, (2 * SIDE, 256), 0)
    freq_y = (2 * line + row // SIDE).astype(jnp.float32)
    freq_z = (row % SIDE).astype(jnp.float32)
    column = lax.broadcasted_iota(jnp.int32, (1, 256), 1)
    quarter = (0.5 * math.pi) ** 2
    for r in range(OWN):
        h, pair = r // PAIRS, r % PAIRS
        y = freq_y / live(extents, first + r, 0)
        z = freq_z / live(extents, first + r, 1)
        across = quarter * (y * y + z * z)
        for chunk in range(4):
            lanes = slice(chunk * 256, chunk * 256 + 256)
            x = (column + chunk * 256).astype(jnp.float32) * (1.0 / 1024.0)
            u = across + quarter * (x * x)
            s = series(u, 9)
            both[0, h, pair, :, lanes] = (2.0 - u * s) * now[h, pair, :, lanes] - previous[h, pair, :, lanes]
            both[1, h, pair, :, lanes] = 0.25 * s


def active_kernel(extents, active):
    first = lax.axis_index("region") * OWN
    line = lax.axis_index("line")
    row = lax.broadcasted_iota(jnp.int32, (2 * SIDE, LANES), 0)
    freq_y = 2 * line + row // SIDE
    freq_z = row % SIDE
    for r in range(OWN):
        inside = (freq_y < extents[0, first + r]) & (freq_z < extents[1, first + r])
        active[r // PAIRS, r % PAIRS] = jnp.where(inside, 1.0, 0.0)


def rows_kernel(tables, to_cells, modes, rows):
    for pair in range(PAIRS):
        even, odd = [None] * 3, [None] * 3
        for source in range(16):
            for which, total in ((0, even), (1, odd)):
                block = modes[source, pair, which * SIDE : (which + 1) * SIDE]
                for e in range(3):
                    at = e * SIDE + 2 * source + which
                    term = tables[pair, at : at + 1] * block
                    total[e] = term if total[e] is None else total[e] + term
        lower = [even[e] + odd[e] for e in range(3)]
        upper = [even[e] - odd[e] for e in range(3)]
        for i, cells in enumerate(z_apply(to_cells[pair], lower + upper)):
            rows[pair, i] = cells


def spread(d):
    return [A1 * d[0] + A2 * d[1] + A3 * d[2], A2 * d[0] + A3 * d[1], A3 * d[0]]


def force_kernel(places, tables, to_modes, masks, own, up, down, out, near, made, sent):
    copies = []
    for pair in range(PAIRS):
        near[pair] = down[pair]
        near[PAIRS + pair] = own[pair]
        near[2 * PAIRS + pair] = up[pair]
    left = left_half((3, SIDE, LANES))
    for pair in range(PAIRS):
        taken = []
        for face in range(2):
            pieces = []
            for half in range(2):
                at = 3 * ((pair * 2 + face) * 2 + half)
                row = 0 if face == 1 else 3
                cells = near[places[at], row : row + 3]
                cells = pltpu.roll(cells, places[at + 1], 1)
                pieces.append(
                    jnp.where(places[at + 2] == half, cells, pltpu.roll(cells, LANES // 2, 2))
                )
            both = jnp.where(left, pieces[0], pieces[1])
            mask = masks[pair, face]
            taken.append(spread([mask * (both[e] - own[pair, 3 * face + e]) for e in range(3)]))
        even = [taken[0][e] + taken[1][e] for e in range(3)]
        odd = [taken[0][e] - taken[1][e] for e in range(3)]
        sixfold = z_apply(to_modes[pair], even + odd)
        for target in range(16):
            for which, parts in ((0, sixfold[:3]), (1, sixfold[3:])):
                value = None
                for e in range(3):
                    at = e * SIDE + 2 * target + which
                    term = tables[pair, at : at + 1] * parts[e]
                    value = term if value is None else value + term
                made[pair, target, which * SIDE : (which + 1) * SIDE] = value
        copies.append(pltpu.make_async_copy(made.at[pair], out.at[:, pair], sent.at[pair]))
        copies[-1].start()
    for copy in copies:
        copy.wait()


def update_kernel(mixed_hbm, active, both, out, mixed, made, arrived, sent):
    left = left_half((2 * SIDE, LANES))
    inward, outward = [], []
    for part in range(2 * PAIRS):
        pair, half = part // 2, part % 2
        source = mixed_hbm.at[pl.ds(half * 8, 8), pair]
        target = out.at[:, pair, :, pl.ds(half * 512, 512)]
        inward.append(pltpu.make_async_copy(source, mixed.at[part], arrived.at[part]))
        outward.append(pltpu.make_async_copy(made.at[part], target, sent.at[part]))
        inward[-1].start()
    for part in range(2 * PAIRS):
        pair, half = part // 2, part % 2
        inward[part].wait()
        for chip in range(4):
            here = slice(chip * LANES, chip * LANES + LANES)
            lanes = slice(half * 512 + chip * LANES, half * 512 + chip * LANES + LANES)
            a = mixed[part, 2 * chip]
            b = mixed[part, 2 * chip + 1]
            one = jnp.where(left, a, pltpu.roll(b, LANES // 2, 1))
            two = jnp.where(left, pltpu.roll(a, LANES // 2, 1), b)
            for h, spectral in ((0, one), (1, two)):
                stepped = both[0, h, pair, :, lanes] + both[1, h, pair, :, lanes] * spectral
                made[part, h, :, here] = jnp.where(active[h, pair] > 0.0, stepped, 0.0)
        outward[part].start()
    for copy in outward:
        copy.wait()


def smem():
    return pl.BlockSpec(memory_space=pltpu.SMEM)


def vmem():
    return pl.BlockSpec(memory_space=pltpu.VMEM)


def hbm():
    return pl.BlockSpec(memory_space=pltpu.HBM)


def cost(flops, nbytes):
    return pl.CostEstimate(flops=flops, bytes_accessed=nbytes, transcendentals=0)


def shards(modes_now, modes_prev, extents, partner, offset):
    f32 = jnp.float32
    extents = extents.T
    now = modes_now.reshape(2, PAIRS, 2 * SIDE, 1024)
    previous = modes_prev.reshape(2, PAIRS, 2 * SIDE, 1024)
    nbytes = now.size * 4
    wide_shape = jax.ShapeDtypeStruct(now.shape, f32)
    packed_shape = jax.ShapeDtypeStruct((16, PAIRS, 2 * SIDE, LANES), f32)
    rows_shape = jax.ShapeDtypeStruct((PAIRS, 6, SIDE, LANES), f32)
    table_shape = jax.ShapeDtypeStruct((PAIRS, 2 * SIDE, LANES), jnp.bfloat16)
    params = pltpu.CompilerParams(vmem_limit_bytes=VMEM_LIMIT)
    wide_parts = pltpu.VMEM((2 * PAIRS, 2, 2 * SIDE, 512), f32)
    packed_parts = pltpu.VMEM((2 * PAIRS, 8, 2 * SIDE, LANES), f32)
    copied_parts = pltpu.SemaphoreType.DMA((2 * PAIRS,))
    packed_scratch = pltpu.VMEM((PAIRS, 16, 2 * SIDE, LANES), f32)
    copied = pltpu.SemaphoreType.DMA((PAIRS,))

    with jax.named_scope("encode"):
        sent = pl.pallas_call(
            encode_kernel,
            out_shape=packed_shape,
            in_specs=[hbm()],
            out_specs=hbm(),
            scratch_shapes=[wide_parts, packed_parts, copied_parts, copied_parts],
            compiler_params=pltpu.CompilerParams(vmem_limit_bytes=ENCODE_LIMIT),
            cost_estimate=cost(10**6, 2 * nbytes),
        )(now)
    held = lax.all_to_all(sent, "line", 0, 0, tiled=True)
    with jax.named_scope("plan"):
        y_tables, to_cells, to_modes, masks, places = pl.pallas_call(
            plan_kernel,
            out_shape=(
                jax.ShapeDtypeStruct((PAIRS, 3 * SIDE, LANES), f32),
                table_shape,
                table_shape,
                jax.ShapeDtypeStruct((PAIRS, 2, SIDE, LANES), f32),
                jax.ShapeDtypeStruct((36,), jnp.int32),
            ),
            in_specs=[smem(), smem(), smem()],
            out_specs=(vmem(), vmem(), vmem(), vmem(), smem()),
            compiler_params=params,
            cost_estimate=cost(10**8, 10**6),
        )(extents, partner, offset)
    with jax.named_scope("rows"):
        rows = pl.pallas_call(
            rows_kernel,
            out_shape=rows_shape,
            in_specs=[vmem()] * 3,
            out_specs=vmem(),
            compiler_params=params,
            cost_estimate=cost(10**7, nbytes),
        )(y_tables, to_cells, held)
    count = lax.axis_size("region")
    up = lax.ppermute(rows, "region", [((i + 1) % count, i) for i in range(count)])
    down = lax.ppermute(rows, "region", [(i, (i + 1) % count) for i in range(count)])
    with jax.named_scope("free"):
        both = pl.pallas_call(
            free_kernel,
            out_shape=jax.ShapeDtypeStruct((2, *now.shape), f32),
            in_specs=[smem(), vmem(), vmem()],
            out_specs=vmem(),
            compiler_params=params,
            cost_estimate=cost(10**9, 4 * nbytes),
        )(extents, *lax.optimization_barrier((now, previous, rows))[:2])
    down, both = lax.optimization_barrier((down, both))
    with jax.named_scope("active"):
        active = pl.pallas_call(
            active_kernel,
            out_shape=jax.ShapeDtypeStruct((2, PAIRS, 2 * SIDE, LANES), f32),
            in_specs=[smem()],
            out_specs=vmem(),
            compiler_params=params,
            cost_estimate=cost(10**9, nbytes),
        )(extents)
    with jax.named_scope("force"):
        forced = pl.pallas_call(
            force_kernel,
            out_shape=packed_shape,
            in_specs=[smem()] + [vmem()] * 6,
            out_specs=hbm(),
            scratch_shapes=[pltpu.VMEM((3 * PAIRS, 6, SIDE, LANES), f32), packed_scratch, copied],
            compiler_params=pltpu.CompilerParams(vmem_limit_bytes=FORCE_LIMIT),
            cost_estimate=cost(10**7, nbytes),
        )(places, y_tables, to_modes, masks, rows, up, down)
    mixed = lax.all_to_all(forced, "line", 0, 0, tiled=True)
    with jax.named_scope("update"):
        result = pl.pallas_call(
            update_kernel,
            out_shape=wide_shape,
            in_specs=[hbm(), vmem(), vmem()],
            out_specs=hbm(),
            scratch_shapes=[packed_parts, wide_parts, copied_parts, copied_parts],
            compiler_params=params,
            cost_estimate=cost(10**7, 4 * nbytes),
        )(mixed, active, both)
    return result.reshape(modes_now.shape)


def solution(mesh):
    return jax.shard_map(
        shards,
        mesh=mesh,
        in_specs=(P("region", "line", None), P("region", "line", None), P(), P(), P()),
        out_specs=P("region", "line", None),
        check_vma=False,
    )
```

```python
import math

import jax
import jax.numpy as jnp
from jax import lax
from jax.experimental import pallas as pl
from jax.experimental.pallas import tpu as pltpu
from jax.sharding import PartitionSpec as P

SIDE = 32
PAIRS = 3
OWN = 6
LANES = 128
A1, A2, A3 = 1.5, -0.15, 1.0 / 90.0
VMEM_LIMIT = 16 * 1024 * 1024
ENCODE_LIMIT = 63 * 1024 * 1024

SERIES = [2.0 * (-1.0) ** k / math.factorial(2 * k + 2) for k in range(10)]


def series(u, terms):
    total = jnp.full_like(u, SERIES[terms - 1])
    for coefficient in SERIES[: terms - 1][::-1]:
        total = total * u + coefficient
    return total


def cosine_entry(freq, cell, live):
    inverse = 1.0 / live
    turn = 4.0 * live
    steps = freq * (2.0 * cell + 1.0)
    steps = steps - turn * jnp.floor((steps + 0.5) * (0.25 * inverse))
    steps = jnp.minimum(steps, turn - steps)
    flip = steps > live
    steps = jnp.where(flip, 2.0 * live - steps, steps)
    angle = (0.5 * math.pi) * (steps * inverse)
    u = angle * angle
    value = 1.0 - 0.5 * u * series(u, 7)
    value = jnp.where(flip, -value, value)
    weight = jnp.sqrt(jnp.where(freq == 0.0, 1.0, 2.0) * inverse)
    return jnp.where((freq < live) & (cell < live), weight * value, 0.0)


def z_table(live_z, to_cells):
    shape = (SIDE, LANES)
    row = lax.broadcasted_iota(jnp.int32, shape, 0).astype(jnp.float32)
    lane = lax.broadcasted_iota(jnp.int32, shape, 1)
    column = (lane % SIDE).astype(jnp.float32)
    freq, cell = (column, row) if to_cells else (row, column)
    table = cosine_entry(freq, cell, jnp.full(shape, live_z, jnp.float32))
    high = table.astype(jnp.bfloat16).astype(jnp.float32)
    return jnp.where(lane < LANES // 2, high, table - high).astype(jnp.bfloat16)


def z_apply(table, parts):
    values = jnp.concatenate(parts, axis=1)
    high = values.astype(jnp.bfloat16)
    low = (values - high.astype(jnp.float32)).astype(jnp.bfloat16)
    stacked = jnp.concatenate([high, low, high, low], axis=0)
    both = jnp.dot(table, stacked, preferred_element_type=jnp.float32)
    left = left_half((SIDE, LANES))
    return [
        jnp.where(
            left,
            both[:SIDE, i * LANES : (i + 1) * LANES],
            both[SIDE:, i * LANES : (i + 1) * LANES],
        )
        for i in range(len(parts))
    ]


def live(extents, rect, which):
    return extents[which, rect].astype(jnp.float32)


def left_half(shape):
    return lax.broadcasted_iota(jnp.int32, shape, len(shape) - 1) < LANES // 2


def encode_kernel(now, out, held, made, arrived, sent):
    left = left_half((2 * SIDE, LANES))
    inward, outward = [], []
    for part in range(2 * PAIRS):
        pair, half = part // 2, part % 2
        source = now.at[:, pair, :, pl.ds(half * 512, 512)]
        target = out.at[pl.ds(half * 8, 8), pair]
        inward.append(pltpu.make_async_copy(source, held.at[part], arrived.at[part]))
        outward.append(pltpu.make_async_copy(made.at[part], target, sent.at[part]))
        inward[-1].start()
    for part in range(2 * PAIRS):
        inward[part].wait()
        for chip in range(4):
            lanes = slice(chip * LANES, chip * LANES + LANES)
            a = held[part, 0, :, lanes]
            b = held[part, 1, :, lanes]
            made[part, 2 * chip] = jnp.where(left, a, pltpu.roll(b, LANES // 2, 1))
            made[part, 2 * chip + 1] = jnp.where(left, pltpu.roll(a, LANES // 2, 1), b)
        outward[part].start()
    for copy in outward:
        copy.wait()


def plan_kernel(extents, partner, offset, y_tables, to_cells, to_modes, masks, places):
    region = lax.axis_index("region")
    count = lax.axis_size("region")
    first = region * OWN
    total = count * OWN
    left = left_half((3 * SIDE, LANES))
    index = lax.broadcasted_iota(jnp.int32, (3 * SIDE, LANES), 0)
    freq = (index % SIDE).astype(jnp.float32)
    cell = (index // SIDE).astype(jnp.float32)
    for pair in range(PAIRS):
        one, two = first + pair, first + pair + PAIRS
        live_y = jnp.where(left, live(extents, one, 0), live(extents, two, 0))
        y_tables[pair] = cosine_entry(freq, cell, live_y)
        for h, rect in ((0, one), (1, two)):
            live_z = live(extents, rect, 1)
            to_cells[pair, h * SIDE : (h + 1) * SIDE] = z_table(live_z, True)
            to_modes[pair, h * SIDE : (h + 1) * SIDE] = z_table(live_z, False)
    lower_of = [jnp.int32(0)] * OWN
    for w in range(3 * OWN):
        rect = lax.rem(first + total + w - OWN, total)
        target = partner[rect] - first
        for r in range(OWN):
            lower_of[r] = jnp.where(target == r, rect, lower_of[r])
    z = lax.broadcasted_iota(jnp.int32, (SIDE, LANES), 0)
    left = left_half((SIDE, LANES))
    for pair in range(PAIRS):
        for face in range(2):
            parts = []
            for half in range(2):
                r = pair + PAIRS * half
                rect = first + r
                if face == 1:
                    other = partner[rect]
                    shift = offset[rect]
                else:
                    other = lower_of[r]
                    shift = -offset[other]
                place = lax.div(other, OWN)
                slot = other - place * OWN
                side = lax.div(slot, PAIRS)
                at = 3 * ((pair * 2 + face) * 2 + half)
                places[at] = lax.rem(place - region + 1 + count, count) * PAIRS + slot - side * PAIRS
                places[at + 1] = lax.rem(shift + SIDE, SIDE)
                places[at + 2] = side
                source = z - shift
                inside = (source >= 0) & (source < extents[1, other]) & (z < extents[1, rect])
                parts.append(jnp.where(inside, 1.0, 0.0))
            masks[pair, face] = jnp.where(left, parts[0], parts[1])


def free_kernel(extents, now, previous, base, gain):
    first = lax.axis_index("region") * OWN
    line = lax.axis_index("line")
    row = lax.broadcasted_iota(jnp.int32, (2 * SIDE, 256), 0)
    freq_y = (2 * line + row // SIDE).astype(jnp.float32)
    freq_z = (row % SIDE).astype(jnp.float32)
    column = lax.broadcasted_iota(jnp.int32, (1, 256), 1)
    quarter = (0.5 * math.pi) ** 2
    for r in range(OWN):
        h, pair = r // PAIRS, r % PAIRS
        live_y = live(extents, first + r, 0)
        live_z = live(extents, first + r, 1)
        y = freq_y / live_y
        z = freq_z / live_z
        across = quarter * (y * y + z * z)
        active = (freq_y < live_y) & (freq_z < live_z)
        for chunk in range(4):
            lanes = slice(chunk * 256, chunk * 256 + 256)
            x = (column + chunk * 256).astype(jnp.float32) * (1.0 / 1024.0)
            u = across + quarter * (x * x)
            s = series(u, 9)
            stepped = (2.0 - u * s) * now[h, pair, :, lanes] - previous[h, pair, :, lanes]
            base[h, pair, :, lanes] = jnp.where(active, stepped, 0.0)
            gain[h, pair, :, lanes] = jnp.where(active, 0.25 * s, 0.0)


def rows_kernel(tables, to_cells, modes, rows):
    for pair in range(PAIRS):
        even, odd = [None] * 3, [None] * 3
        for source in range(16):
            for which, total in ((0, even), (1, odd)):
                block = modes[source, pair, which * SIDE : (which + 1) * SIDE]
                for e in range(3):
                    at = e * SIDE + 2 * source + which
                    term = tables[pair, at : at + 1] * block
                    total[e] = term if total[e] is None else total[e] + term
        lower = [even[e] + odd[e] for e in range(3)]
        upper = [even[e] - odd[e] for e in range(3)]
        for i, cells in enumerate(z_apply(to_cells[pair], lower + upper)):
            rows[pair, i] = cells


def spread(d):
    return [A1 * d[0] + A2 * d[1] + A3 * d[2], A2 * d[0] + A3 * d[1], A3 * d[0]]


def force_kernel(places, tables, to_modes, masks, own, up, down, out, near):
    for pair in range(PAIRS):
        near[pair] = down[pair]
        near[PAIRS + pair] = own[pair]
        near[2 * PAIRS + pair] = up[pair]
    left = left_half((3, SIDE, LANES))
    for pair in range(PAIRS):
        taken = []
        for face in range(2):
            pieces = []
            for half in range(2):
                at = 3 * ((pair * 2 + face) * 2 + half)
                row = 0 if face == 1 else 3
                cells = near[places[at], row : row + 3]
                cells = pltpu.roll(cells, places[at + 1], 1)
                pieces.append(
                    jnp.where(places[at + 2] == half, cells, pltpu.roll(cells, LANES // 2, 2))
                )
            both = jnp.where(left, pieces[0], pieces[1])
            mask = masks[pair, face]
            taken.append(spread([mask * (both[e] - own[pair, 3 * face + e]) for e in range(3)]))
        even = [taken[0][e] + taken[1][e] for e in range(3)]
        odd = [taken[0][e] - taken[1][e] for e in range(3)]
        sixfold = z_apply(to_modes[pair], even + odd)
        for target in range(16):
            for which, parts in ((0, sixfold[:3]), (1, sixfold[3:])):
                value = None
                for e in range(3):
                    at = e * SIDE + 2 * target + which
                    term = tables[pair, at : at + 1] * parts[e]
                    value = term if value is None else value + term
                out[target, pair, which * SIDE : (which + 1) * SIDE] = value


def update_kernel(mixed, base, gain, out, made, sent):
    left = left_half((2 * SIDE, LANES))
    copies = []
    for pair in range(PAIRS):
        for chip in range(8):
            lanes = slice(chip * LANES, chip * LANES + LANES)
            a = mixed[2 * chip, pair]
            b = mixed[2 * chip + 1, pair]
            one = jnp.where(left, a, pltpu.roll(b, LANES // 2, 1))
            two = jnp.where(left, pltpu.roll(a, LANES // 2, 1), b)
            for h, spectral in ((0, one), (1, two)):
                made[pair, h, :, lanes] = base[h, pair, :, lanes] + gain[h, pair, :, lanes] * spectral
        copies.append(pltpu.make_async_copy(made.at[pair], out.at[:, pair], sent.at[pair]))
        copies[-1].start()
    for copy in copies:
        copy.wait()


def smem():
    return pl.BlockSpec(memory_space=pltpu.SMEM)


def vmem():
    return pl.BlockSpec(memory_space=pltpu.VMEM)


def hbm():
    return pl.BlockSpec(memory_space=pltpu.HBM)


def cost(flops, nbytes):
    return pl.CostEstimate(flops=flops, bytes_accessed=nbytes, transcendentals=0)


def shards(modes_now, modes_prev, extents, partner, offset):
    f32 = jnp.float32
    extents = extents.T
    now = modes_now.reshape(2, PAIRS, 2 * SIDE, 1024)
    previous = modes_prev.reshape(2, PAIRS, 2 * SIDE, 1024)
    nbytes = now.size * 4
    wide_shape = jax.ShapeDtypeStruct(now.shape, f32)
    packed_shape = jax.ShapeDtypeStruct((16, PAIRS, 2 * SIDE, LANES), f32)
    rows_shape = jax.ShapeDtypeStruct((PAIRS, 6, SIDE, LANES), f32)
    table_shape = jax.ShapeDtypeStruct((PAIRS, 2 * SIDE, LANES), jnp.bfloat16)
    params = pltpu.CompilerParams(vmem_limit_bytes=VMEM_LIMIT)
    wide_parts = pltpu.VMEM((2 * PAIRS, 2, 2 * SIDE, 512), f32)
    packed_parts = pltpu.VMEM((2 * PAIRS, 8, 2 * SIDE, LANES), f32)
    copied_parts = pltpu.SemaphoreType.DMA((2 * PAIRS,))

    with jax.named_scope("encode"):
        sent = pl.pallas_call(
            encode_kernel,
            out_shape=packed_shape,
            in_specs=[hbm()],
            out_specs=hbm(),
            scratch_shapes=[wide_parts, packed_parts, copied_parts, copied_parts],
            compiler_params=pltpu.CompilerParams(vmem_limit_bytes=ENCODE_LIMIT),
            cost_estimate=cost(10**6, 2 * nbytes),
        )(now)
    held = lax.all_to_all(sent, "line", 0, 0, tiled=True)
    with jax.named_scope("plan"):
        y_tables, to_cells, to_modes, masks, places = pl.pallas_call(
            plan_kernel,
            out_shape=(
                jax.ShapeDtypeStruct((PAIRS, 3 * SIDE, LANES), f32),
                table_shape,
                table_shape,
                jax.ShapeDtypeStruct((PAIRS, 2, SIDE, LANES), f32),
                jax.ShapeDtypeStruct((36,), jnp.int32),
            ),
            in_specs=[smem(), smem(), smem()],
            out_specs=(vmem(), vmem(), vmem(), vmem(), smem()),
            compiler_params=params,
            cost_estimate=cost(10**8, 10**6),
        )(extents, partner, offset)
    with jax.named_scope("rows"):
        rows = pl.pallas_call(
            rows_kernel,
            out_shape=rows_shape,
            in_specs=[vmem()] * 3,
            out_specs=vmem(),
            compiler_params=params,
            cost_estimate=cost(10**7, nbytes),
        )(y_tables, to_cells, held)
    count = lax.axis_size("region")
    up = lax.ppermute(rows, "region", [((i + 1) % count, i) for i in range(count)])
    down = lax.ppermute(rows, "region", [(i, (i + 1) % count) for i in range(count)])
    with jax.named_scope("free"):
        base, gain = pl.pallas_call(
            free_kernel,
            out_shape=(wide_shape, wide_shape),
            in_specs=[smem(), vmem(), vmem()],
            out_specs=(vmem(), vmem()),
            compiler_params=params,
            cost_estimate=cost(10**9, 4 * nbytes),
        )(extents, *lax.optimization_barrier((now, previous, rows))[:2])
    down, base, gain = lax.optimization_barrier((down, base, gain))
    with jax.named_scope("force"):
        forced = pl.pallas_call(
            force_kernel,
            out_shape=packed_shape,
            in_specs=[smem()] + [vmem()] * 6,
            out_specs=vmem(),
            scratch_shapes=[pltpu.VMEM((3 * PAIRS, 6, SIDE, LANES), f32)],
            compiler_params=params,
            cost_estimate=cost(10**7, nbytes),
        )(places, y_tables, to_modes, masks, rows, up, down)
    mixed = lax.all_to_all(forced, "line", 0, 0, tiled=True)
    with jax.named_scope("update"):
        result = pl.pallas_call(
            update_kernel,
            out_shape=wide_shape,
            in_specs=[vmem()] * 3,
            out_specs=hbm(),
            scratch_shapes=[pltpu.VMEM((PAIRS, 2, 2 * SIDE, 1024), f32), pltpu.SemaphoreType.DMA((PAIRS,))],
            compiler_params=params,
            cost_estimate=cost(10**7, 4 * nbytes),
        )(mixed, base, gain)
    return result.reshape(modes_now.shape)


def solution(mesh):
    return jax.shard_map(
        shards,
        mesh=mesh,
        in_specs=(P("region", "line", None), P("region", "line", None), P(), P(), P()),
        out_specs=P("region", "line", None),
        check_vma=False,
    )
```

```python
import functools
import math

import jax
import jax.numpy as jnp
from jax import lax
from jax.experimental import pallas as pl
from jax.experimental.pallas import tpu as pltpu
from jax.sharding import PartitionSpec as P

SIDE = 32
PAIRS = 3
OWN = 6
LANES = 128
A1, A2, A3 = 1.5, -0.15, 1.0 / 90.0
VMEM_LIMIT = 16 * 1024 * 1024
ENCODE_LIMIT = 63 * 1024 * 1024

SERIES = [2.0 * (-1.0) ** k / math.factorial(2 * k + 2) for k in range(10)]


def series(u, terms):
    total = jnp.full_like(u, SERIES[terms - 1])
    for coefficient in SERIES[: terms - 1][::-1]:
        total = total * u + coefficient
    return total


def cosine_entry(freq, cell, live):
    inverse = 1.0 / live
    turn = 4.0 * live
    steps = freq * (2.0 * cell + 1.0)
    steps = steps - turn * jnp.floor((steps + 0.5) * (0.25 * inverse))
    steps = jnp.minimum(steps, turn - steps)
    flip = steps > live
    steps = jnp.where(flip, 2.0 * live - steps, steps)
    angle = (0.5 * math.pi) * (steps * inverse)
    u = angle * angle
    value = 1.0 - 0.5 * u * series(u, 7)
    value = jnp.where(flip, -value, value)
    weight = jnp.sqrt(jnp.where(freq == 0.0, 1.0, 2.0) * inverse)
    return jnp.where((freq < live) & (cell < live), weight * value, 0.0)


def z_table(live_z, to_cells):
    shape = (SIDE, LANES)
    row = lax.broadcasted_iota(jnp.int32, shape, 0).astype(jnp.float32)
    lane = lax.broadcasted_iota(jnp.int32, shape, 1)
    column = (lane % SIDE).astype(jnp.float32)
    freq, cell = (column, row) if to_cells else (row, column)
    table = cosine_entry(freq, cell, jnp.full(shape, live_z, jnp.float32))
    high = table.astype(jnp.bfloat16).astype(jnp.float32)
    return jnp.where(lane < LANES // 2, high, table - high).astype(jnp.bfloat16)


def z_apply(table, parts):
    values = jnp.concatenate(parts, axis=1)
    high = values.astype(jnp.bfloat16)
    low = (values - high.astype(jnp.float32)).astype(jnp.bfloat16)
    stacked = jnp.concatenate([high, low, high, low], axis=0)
    both = jnp.dot(table, stacked, preferred_element_type=jnp.float32)
    first = even_group((SIDE, LANES))
    return [
        jnp.where(
            first,
            both[:SIDE, i * LANES : (i + 1) * LANES],
            both[SIDE:, i * LANES : (i + 1) * LANES],
        )
        for i in range(len(parts))
    ]


def live(extents, rect, which):
    return extents[which, rect].astype(jnp.float32)


def lanes_of(shape):
    return lax.broadcasted_iota(jnp.int32, shape, len(shape) - 1)


def left_half(shape):
    return lanes_of(shape) < LANES // 2


def even_group(shape):
    return (lanes_of(shape) // SIDE) % 2 == 0


def regroup(tiles):
    left, even = left_half(tiles[0].shape), even_group(tiles[0].shape)
    half = [None] * 4
    for i in range(2):
        a, b = tiles[i], tiles[i + 2]
        half[i] = jnp.where(left, a, pltpu.roll(b, 64, 1))
        half[i + 2] = jnp.where(left, pltpu.roll(a, 64, 1), b)
    out = [None] * 4
    for i in (0, 2):
        a, b = half[i], half[i + 1]
        out[i] = jnp.where(even, a, pltpu.roll(b, 32, 1))
        out[i + 1] = jnp.where(even, pltpu.roll(a, 96, 1), b)
    return out


def encode_kernel(part, now, out, held, made, arrived, sent):
    inward = [
        pltpu.make_async_copy(now.at[:, i], held.at[i], arrived.at[i]) for i in range(PAIRS)
    ]
    outward = [
        pltpu.make_async_copy(made.at[i], out.at[:, i], sent.at[i]) for i in range(PAIRS)
    ]
    for copy in inward:
        copy.start()
    for pair in range(PAIRS):
        inward[pair].wait()
        for chip in range(8):
            lanes = slice(chip * LANES, chip * LANES + LANES)
            tiles = [
                held[pair, h, parity * SIDE : (parity + 1) * SIDE, lanes]
                for parity in range(2)
                for h in range(2)
            ]
            tiles = regroup(tiles)
            for core in range(2):
                made[pair, 2 * chip + core] = tiles[2 * core + part]
        outward[pair].start()
    for copy in outward:
        copy.wait()


def plan_kernel(extents, partner, offset, y_tables, to_cells, to_modes, masks, places):
    region = lax.axis_index("region")
    count = lax.axis_size("region")
    first = region * OWN
    total = count * OWN
    shape = (48, LANES)
    index = lax.broadcasted_iota(jnp.int32, shape, 0)
    parity = lanes_of(shape) // (2 * SIDE)
    even = even_group(shape)
    freq = (2 * (index % 16) + parity).astype(jnp.float32)
    cell = (index // 16).astype(jnp.float32)
    for pair in range(PAIRS):
        one, two = first + pair, first + pair + PAIRS
        live_y = jnp.where(even, live(extents, one, 0), live(extents, two, 0))
        y_tables[pair] = cosine_entry(freq, cell, live_y)
        for h, rect in ((0, one), (1, two)):
            live_z = live(extents, rect, 1)
            to_cells[pair, h * SIDE : (h + 1) * SIDE] = z_table(live_z, True)
            to_modes[pair, h * SIDE : (h + 1) * SIDE] = z_table(live_z, False)
    lower_of = [jnp.int32(0)] * OWN
    for w in range(3 * OWN):
        rect = lax.rem(first + total + w - OWN, total)
        target = partner[rect] - first
        for r in range(OWN):
            lower_of[r] = jnp.where(target == r, rect, lower_of[r])
    z = lax.broadcasted_iota(jnp.int32, (SIDE, LANES), 0)
    group = lanes_of((SIDE, LANES)) // SIDE
    for pair in range(PAIRS):
        mask = jnp.zeros((SIDE, LANES), jnp.float32)
        for face in range(2):
            for half in range(2):
                r = pair + PAIRS * half
                rect = first + r
                if face == 1:
                    other = partner[rect]
                    shift = offset[rect]
                else:
                    other = lower_of[r]
                    shift = -offset[other]
                place = lax.div(other, OWN)
                slot = other - place * OWN
                side = lax.div(slot, PAIRS)
                to = 2 * face + half
                at = 3 * (4 * pair + to)
                places[at] = lax.rem(place - region + 1 + count, count) * PAIRS + slot - side * PAIRS
                places[at + 1] = lax.rem(shift + SIDE, SIDE)
                places[at + 2] = lax.rem((to - 2 * (1 - face) - side + 4) * SIDE, LANES)
                source = z - shift
                inside = (source >= 0) & (source < extents[1, other]) & (z < extents[1, rect])
                mask = jnp.where((group == to) & inside, 1.0, mask)
        masks[pair] = mask


def free_kernel(extents, now, previous, base, gain):
    first = lax.axis_index("region") * OWN
    line = lax.axis_index("line")
    row = lax.broadcasted_iota(jnp.int32, (2 * SIDE, 256), 0)
    freq_y = (2 * line + row // SIDE).astype(jnp.float32)
    freq_z = (row % SIDE).astype(jnp.float32)
    column = lax.broadcasted_iota(jnp.int32, (1, 256), 1)
    quarter = (0.5 * math.pi) ** 2
    for r in range(OWN):
        h, pair = r // PAIRS, r % PAIRS
        live_y = live(extents, first + r, 0)
        live_z = live(extents, first + r, 1)
        y = freq_y / live_y
        z = freq_z / live_z
        across = quarter * (y * y + z * z)
        active = (freq_y < live_y) & (freq_z < live_z)
        for chunk in range(4):
            lanes = slice(chunk * 256, chunk * 256 + 256)
            x = (column + chunk * 256).astype(jnp.float32) * (1.0 / 1024.0)
            u = across + quarter * (x * x)
            s = series(u, 9)
            stepped = (2.0 - u * s) * now[h, pair, :, lanes] - previous[h, pair, :, lanes]
            base[h, pair, :, lanes] = jnp.where(active, stepped, 0.0)
            gain[h, pair, :, lanes] = jnp.where(active, 0.25 * s, 0.0)


def fold(packed):
    swapped = pltpu.roll(packed, LANES // 2, 1)
    return jnp.where(left_half(packed.shape), packed + swapped, swapped - packed)


def rows_kernel(tables, to_cells, modes, rows):
    for pair in range(PAIRS):
        totals = [None] * 3
        for source in range(16):
            block = modes[source, pair]
            for e in range(3):
                at = e * 16 + source
                term = tables[pair, at : at + 1] * block
                totals[e] = term if totals[e] is None else totals[e] + term
        for e, cells in enumerate(z_apply(to_cells[pair], [fold(t) for t in totals])):
            rows[pair, e] = cells


def spread(d):
    return [A1 * d[0] + A2 * d[1] + A3 * d[2], A2 * d[0] + A3 * d[1], A3 * d[0]]


def force_kernel(places, tables, to_modes, masks, own, up, down, out, near):
    for pair in range(PAIRS):
        near[pair] = down[pair]
        near[PAIRS + pair] = own[pair]
        near[2 * PAIRS + pair] = up[pair]
    group = lanes_of((3, SIDE, LANES)) // SIDE
    for pair in range(PAIRS):
        both = None
        for to in range(4):
            at = 3 * (4 * pair + to)
            cells = pltpu.roll(near[places[at]], places[at + 1], 1)
            cells = pltpu.roll(cells, places[at + 2], 2)
            both = cells if both is None else jnp.where(group == to, cells, both)
        mask = masks[pair]
        parts = spread([mask * (both[e] - own[pair, e]) for e in range(3)])
        parts = z_apply(to_modes[pair], [fold(part) for part in parts])
        for target in range(16):
            value = None
            for e in range(3):
                at = e * 16 + target
                term = tables[pair, at : at + 1] * parts[e]
                value = term if value is None else value + term
            out[target, pair] = value


def update_kernel(mixed_one, mixed_two, base, gain, out, made, sent):
    copies = []
    for pair in range(PAIRS):
        for chip in range(8):
            lanes = slice(chip * LANES, chip * LANES + LANES)
            tiles = regroup(
                [mixed[2 * chip + core, pair] for core in range(2) for mixed in (mixed_one, mixed_two)]
            )
            for parity in range(2):
                modes = slice(parity * SIDE, parity * SIDE + SIDE)
                for h in range(2):
                    made[pair, h, modes, lanes] = (
                        base[h, pair, modes, lanes]
                        + gain[h, pair, modes, lanes] * tiles[2 * parity + h]
                    )
        copies.append(pltpu.make_async_copy(made.at[pair], out.at[:, pair], sent.at[pair]))
        copies[-1].start()
    for copy in copies:
        copy.wait()


def smem():
    return pl.BlockSpec(memory_space=pltpu.SMEM)


def vmem():
    return pl.BlockSpec(memory_space=pltpu.VMEM)


def hbm():
    return pl.BlockSpec(memory_space=pltpu.HBM)


def cost(flops, nbytes):
    return pl.CostEstimate(flops=flops, bytes_accessed=nbytes, transcendentals=0)


def shards(modes_now, modes_prev, extents, partner, offset):
    f32 = jnp.float32
    extents = extents.T
    now = modes_now.reshape(2, PAIRS, 2 * SIDE, 1024)
    previous = modes_prev.reshape(2, PAIRS, 2 * SIDE, 1024)
    nbytes = now.size * 4
    wide_shape = jax.ShapeDtypeStruct(now.shape, f32)
    packed_shape = jax.ShapeDtypeStruct((16, PAIRS, SIDE, LANES), f32)
    rows_shape = jax.ShapeDtypeStruct((PAIRS, 3, SIDE, LANES), f32)
    table_shape = jax.ShapeDtypeStruct((PAIRS, 2 * SIDE, LANES), jnp.bfloat16)
    params = pltpu.CompilerParams(vmem_limit_bytes=VMEM_LIMIT)
    wide_scratch = pltpu.VMEM((PAIRS, 2, 2 * SIDE, 1024), f32)
    copied = pltpu.SemaphoreType.DMA((PAIRS,))
    count = lax.axis_size("region")
    upward = [((i + 1) % count, i) for i in range(count)]
    downward = [(i, (i + 1) % count) for i in range(count)]

    with jax.named_scope("plan"):
        y_tables, to_cells, to_modes, masks, places = pl.pallas_call(
            plan_kernel,
            out_shape=(
                jax.ShapeDtypeStruct((PAIRS, 48, LANES), f32),
                table_shape,
                table_shape,
                jax.ShapeDtypeStruct((PAIRS, SIDE, LANES), f32),
                jax.ShapeDtypeStruct((36,), jnp.int32),
            ),
            in_specs=[smem(), smem(), smem()],
            out_specs=(vmem(), vmem(), vmem(), vmem(), smem()),
            compiler_params=params,
            cost_estimate=cost(10**8, 10**6),
        )(extents, partner, offset)

    def encode(part):
        with jax.named_scope("encode"):
            return pl.pallas_call(
                functools.partial(encode_kernel, part),
                out_shape=packed_shape,
                in_specs=[hbm()],
                out_specs=hbm(),
                scratch_shapes=[
                    wide_scratch,
                    pltpu.VMEM((PAIRS, 16, SIDE, LANES), f32),
                    copied,
                    copied,
                ],
                compiler_params=pltpu.CompilerParams(vmem_limit_bytes=ENCODE_LIMIT),
                cost_estimate=cost(10**6, 2 * nbytes),
            )(now)

    def rows_of(held):
        with jax.named_scope("rows"):
            return pl.pallas_call(
                rows_kernel,
                out_shape=rows_shape,
                in_specs=[vmem()] * 3,
                out_specs=vmem(),
                compiler_params=params,
                cost_estimate=cost(10**7, nbytes),
            )(y_tables, to_cells, held)

    def force(rows, up, down):
        with jax.named_scope("force"):
            return pl.pallas_call(
                force_kernel,
                out_shape=packed_shape,
                in_specs=[smem()] + [vmem()] * 6,
                out_specs=vmem(),
                scratch_shapes=[pltpu.VMEM((3 * PAIRS, 3, SIDE, LANES), f32)],
                compiler_params=params,
                cost_estimate=cost(10**7, nbytes),
            )(places, y_tables, to_modes, masks, rows, up, down)

    def exchange(blocks):
        return lax.all_to_all(blocks, "line", 0, 0, tiled=True)

    def halo(rows):
        return lax.ppermute(rows, "region", upward), lax.ppermute(rows, "region", downward)

    sent_one = encode(0)
    held_one = exchange(sent_one)
    sent_two = encode(1)
    held_two = exchange(sent_two)
    rows_one = rows_of(held_one)
    up_one, down_one = halo(rows_one)
    with jax.named_scope("free"):
        base, gain = pl.pallas_call(
            free_kernel,
            out_shape=(wide_shape, wide_shape),
            in_specs=[smem(), vmem(), vmem()],
            out_specs=(vmem(), vmem()),
            compiler_params=params,
            cost_estimate=cost(10**9, 4 * nbytes),
        )(extents, *lax.optimization_barrier((now, previous, rows_one))[:2])
    down_one, base, gain = lax.optimization_barrier((down_one, base, gain))
    mixed_one = exchange(force(rows_one, up_one, down_one))
    rows_two = rows_of(held_two)
    up_two, down_two = halo(rows_two)
    mixed_two = exchange(force(rows_two, up_two, down_two))
    with jax.named_scope("update"):
        result = pl.pallas_call(
            update_kernel,
            out_shape=wide_shape,
            in_specs=[vmem()] * 4,
            out_specs=hbm(),
            scratch_shapes=[wide_scratch, copied],
            compiler_params=params,
            cost_estimate=cost(10**7, 4 * nbytes),
        )(mixed_one, mixed_two, base, gain)
    return result.reshape(modes_now.shape)


def solution(mesh):
    return jax.shard_map(
        shards,
        mesh=mesh,
        in_specs=(P("region", "line", None), P("region", "line", None), P(), P(), P()),
        out_specs=P("region", "line", None),
        check_vma=False,
    )
```

```python
import functools
import math

import jax
import jax.numpy as jnp
from jax import lax
from jax.experimental import pallas as pl
from jax.experimental.pallas import tpu as pltpu
from jax.sharding import PartitionSpec as P

SIDE = 32
PAIRS = 3
OWN = 6
LANES = 128
A1, A2, A3 = 1.5, -0.15, 1.0 / 90.0
VMEM_LIMIT = 16 * 1024 * 1024
ENCODE_LIMIT = 63 * 1024 * 1024
FREE_LIMIT = 52 * 1024 * 1024

SERIES = [2.0 * (-1.0) ** k / math.factorial(2 * k + 2) for k in range(10)]


def series(u, terms):
    total = jnp.full_like(u, SERIES[terms - 1])
    for coefficient in SERIES[: terms - 1][::-1]:
        total = total * u + coefficient
    return total


def cosine_entry(freq, cell, live):
    inverse = 1.0 / live
    turn = 4.0 * live
    steps = freq * (2.0 * cell + 1.0)
    steps = steps - turn * jnp.floor((steps + 0.5) * (0.25 * inverse))
    steps = jnp.minimum(steps, turn - steps)
    flip = steps > live
    steps = jnp.where(flip, 2.0 * live - steps, steps)
    angle = (0.5 * math.pi) * (steps * inverse)
    u = angle * angle
    value = 1.0 - 0.5 * u * series(u, 7)
    value = jnp.where(flip, -value, value)
    weight = jnp.sqrt(jnp.where(freq == 0.0, 1.0, 2.0) * inverse)
    return jnp.where((freq < live) & (cell < live), weight * value, 0.0)


def z_table(live_z, to_cells):
    shape = (SIDE, LANES)
    row = lax.broadcasted_iota(jnp.int32, shape, 0).astype(jnp.float32)
    lane = lax.broadcasted_iota(jnp.int32, shape, 1)
    column = (lane % SIDE).astype(jnp.float32)
    freq, cell = (column, row) if to_cells else (row, column)
    table = cosine_entry(freq, cell, jnp.full(shape, live_z, jnp.float32))
    high = table.astype(jnp.bfloat16).astype(jnp.float32)
    return jnp.where(lane < LANES // 2, high, table - high).astype(jnp.bfloat16)


def z_apply(table, parts):
    values = jnp.concatenate(parts, axis=1)
    high = values.astype(jnp.bfloat16)
    low = (values - high.astype(jnp.float32)).astype(jnp.bfloat16)
    stacked = jnp.concatenate([high, low, high, low], axis=0)
    both = jnp.dot(table, stacked, preferred_element_type=jnp.float32)
    first = even_group((SIDE, LANES))
    return [
        jnp.where(
            first,
            both[:SIDE, i * LANES : (i + 1) * LANES],
            both[SIDE:, i * LANES : (i + 1) * LANES],
        )
        for i in range(len(parts))
    ]


def live(extents, rect, which):
    return extents[which, rect].astype(jnp.float32)


def lanes_of(shape):
    return lax.broadcasted_iota(jnp.int32, shape, len(shape) - 1)


def left_half(shape):
    return lanes_of(shape) < LANES // 2


def even_group(shape):
    return (lanes_of(shape) // SIDE) % 2 == 0


def regroup(tiles, wanted=range(4)):
    group = lanes_of(tiles[0].shape) // SIDE
    at = [group == i for i in range(3)]

    def pick(four):
        return jnp.where(
            at[0], four[0], jnp.where(at[1], four[1], jnp.where(at[2], four[2], four[3]))
        )

    turned = []
    for k in range(4):
        diagonal = pick([tiles[(g + k) % 4] for g in range(4)])
        turned.append(pltpu.roll(diagonal, k * SIDE, 1) if k else diagonal)
    return [pick([turned[(q - g) % 4] for q in range(4)]) for g in wanted]


def encode_kernel(part, now, out, held, made, arrived, sent):
    inward = [
        pltpu.make_async_copy(now.at[:, i], held.at[i], arrived.at[i]) for i in range(PAIRS)
    ]
    outward = [
        pltpu.make_async_copy(made.at[i], out.at[:, i], sent.at[i]) for i in range(PAIRS)
    ]
    for copy in inward:
        copy.start()
    for pair in range(PAIRS):
        inward[pair].wait()
        for chip in range(8):
            lanes = slice(chip * LANES, chip * LANES + LANES)
            tiles = [
                held[pair, h, parity * SIDE : (parity + 1) * SIDE, lanes]
                for parity in range(2)
                for h in range(2)
            ]
            for core, tile in enumerate(regroup(tiles, (part, 2 + part))):
                made[pair, 2 * chip + core] = tile
        outward[pair].start()
    for copy in outward:
        copy.wait()


def plan_kernel(extents, partner, offset, y_tables, to_cells, to_modes, masks, places):
    region = lax.axis_index("region")
    count = lax.axis_size("region")
    first = region * OWN
    total = count * OWN
    shape = (48, LANES)
    index = lax.broadcasted_iota(jnp.int32, shape, 0)
    parity = lanes_of(shape) // (2 * SIDE)
    even = even_group(shape)
    freq = (2 * (index % 16) + parity).astype(jnp.float32)
    cell = (index // 16).astype(jnp.float32)
    for pair in range(PAIRS):
        one, two = first + pair, first + pair + PAIRS
        live_y = jnp.where(even, live(extents, one, 0), live(extents, two, 0))
        y_tables[pair] = cosine_entry(freq, cell, live_y)
        for h, rect in ((0, one), (1, two)):
            live_z = live(extents, rect, 1)
            to_cells[pair, h * SIDE : (h + 1) * SIDE] = z_table(live_z, True)
            to_modes[pair, h * SIDE : (h + 1) * SIDE] = z_table(live_z, False)
    lower_of = [jnp.int32(0)] * OWN
    for w in range(3 * OWN):
        rect = lax.rem(first + total + w - OWN, total)
        target = partner[rect] - first
        for r in range(OWN):
            lower_of[r] = jnp.where(target == r, rect, lower_of[r])
    z = lax.broadcasted_iota(jnp.int32, (SIDE, LANES), 0)
    group = lanes_of((SIDE, LANES)) // SIDE
    for pair in range(PAIRS):
        mask = jnp.zeros((SIDE, LANES), jnp.float32)
        for face in range(2):
            for half in range(2):
                r = pair + PAIRS * half
                rect = first + r
                if face == 1:
                    other = partner[rect]
                    shift = offset[rect]
                else:
                    other = lower_of[r]
                    shift = -offset[other]
                place = lax.div(other, OWN)
                slot = other - place * OWN
                side = lax.div(slot, PAIRS)
                to = 2 * face + half
                at = 3 * (4 * pair + to)
                places[at] = lax.rem(place - region + 1 + count, count) * PAIRS + slot - side * PAIRS
                places[at + 1] = lax.rem(shift + SIDE, SIDE)
                places[at + 2] = lax.rem((to - 2 * (1 - face) - side + 4) * SIDE, LANES)
                source = z - shift
                inside = (source >= 0) & (source < extents[1, other]) & (z < extents[1, rect])
                mask = jnp.where((group == to) & inside, 1.0, mask)
        masks[pair] = mask


def free_kernel(extents, now_hbm, previous_hbm, base_hbm, gain_hbm, now, previous, base, gain, copied):
    inward, outward = [], []
    for h in range(2):
        inward.append(
            (
                pltpu.make_async_copy(now_hbm.at[h], now.at[h], copied.at[h, 0]),
                pltpu.make_async_copy(previous_hbm.at[h], previous.at[h], copied.at[h, 1]),
            )
        )
        outward.append(
            (
                pltpu.make_async_copy(base.at[h], base_hbm.at[h], copied.at[h, 2]),
                pltpu.make_async_copy(gain.at[h], gain_hbm.at[h], copied.at[h, 3]),
            )
        )
        for copy in inward[h]:
            copy.start()
    first = lax.axis_index("region") * OWN
    line = lax.axis_index("line")
    row = lax.broadcasted_iota(jnp.int32, (2 * SIDE, 256), 0)
    freq_y = (2 * line + row // SIDE).astype(jnp.float32)
    freq_z = (row % SIDE).astype(jnp.float32)
    column = lax.broadcasted_iota(jnp.int32, (1, 256), 1)
    quarter = (0.5 * math.pi) ** 2
    for r in range(OWN):
        h, pair = r // PAIRS, r % PAIRS
        if pair == 0:
            for copy in inward[h]:
                copy.wait()
        live_y = live(extents, first + r, 0)
        live_z = live(extents, first + r, 1)
        y = freq_y / live_y
        z = freq_z / live_z
        across = quarter * (y * y + z * z)
        active = (freq_y < live_y) & (freq_z < live_z)
        for chunk in range(4):
            lanes = slice(chunk * 256, chunk * 256 + 256)
            x = (column + chunk * 256).astype(jnp.float32) * (1.0 / 1024.0)
            u = across + quarter * (x * x)
            s = series(u, 9)
            stepped = (2.0 - u * s) * now[h, pair, :, lanes] - previous[h, pair, :, lanes]
            base[h, pair, :, lanes] = jnp.where(active, stepped, 0.0)
            gain[h, pair, :, lanes] = jnp.where(active, 0.25 * s, 0.0)
        if pair == PAIRS - 1:
            for copy in outward[h]:
                copy.start()
    for copies in outward:
        for copy in copies:
            copy.wait()


def fold(packed):
    swapped = pltpu.roll(packed, LANES // 2, 1)
    return jnp.where(left_half(packed.shape), packed + swapped, swapped - packed)


def rows_kernel(tables, to_cells, modes, rows):
    for pair in range(PAIRS):
        totals = [None] * 3
        for source in range(16):
            block = modes[source, pair]
            for e in range(3):
                at = e * 16 + source
                term = tables[pair, at : at + 1] * block
                totals[e] = term if totals[e] is None else totals[e] + term
        for e, cells in enumerate(z_apply(to_cells[pair], [fold(t) for t in totals])):
            rows[pair, e] = cells


def spread(d):
    return [A1 * d[0] + A2 * d[1] + A3 * d[2], A2 * d[0] + A3 * d[1], A3 * d[0]]


def force_kernel(places, tables, to_modes, masks, own, up, down, out, near):
    for pair in range(PAIRS):
        near[pair] = down[pair]
        near[PAIRS + pair] = own[pair]
        near[2 * PAIRS + pair] = up[pair]
    group = lanes_of((3, SIDE, LANES)) // SIDE
    for pair in range(PAIRS):
        both = None
        for to in range(4):
            at = 3 * (4 * pair + to)
            cells = pltpu.roll(near[places[at]], places[at + 1], 1)
            cells = pltpu.roll(cells, places[at + 2], 2)
            both = cells if both is None else jnp.where(group == to, cells, both)
        mask = masks[pair]
        parts = spread([mask * (both[e] - own[pair, e]) for e in range(3)])
        parts = z_apply(to_modes[pair], [fold(part) for part in parts])
        for target in range(16):
            value = None
            for e in range(3):
                at = e * 16 + target
                term = tables[pair, at : at + 1] * parts[e]
                value = term if value is None else value + term
            out[target, pair] = value


def update_kernel(mixed_one, mixed_two, base, gain, out, made, sent):
    copies = []
    for pair in range(PAIRS):
        for chip in range(8):
            lanes = slice(chip * LANES, chip * LANES + LANES)
            tiles = regroup(
                [mixed[2 * chip + core, pair] for core in range(2) for mixed in (mixed_one, mixed_two)]
            )
            for parity in range(2):
                modes = slice(parity * SIDE, parity * SIDE + SIDE)
                for h in range(2):
                    made[pair, h, modes, lanes] = (
                        base[h, pair, modes, lanes]
                        + gain[h, pair, modes, lanes] * tiles[2 * parity + h]
                    )
        copies.append(pltpu.make_async_copy(made.at[pair], out.at[:, pair], sent.at[pair]))
        copies[-1].start()
    for copy in copies:
        copy.wait()


def smem():
    return pl.BlockSpec(memory_space=pltpu.SMEM)


def vmem():
    return pl.BlockSpec(memory_space=pltpu.VMEM)


def hbm():
    return pl.BlockSpec(memory_space=pltpu.HBM)


def cost(flops, nbytes):
    return pl.CostEstimate(flops=flops, bytes_accessed=nbytes, transcendentals=0)


def shards(modes_now, modes_prev, extents, partner, offset):
    f32 = jnp.float32
    extents = extents.T
    now = modes_now.reshape(2, PAIRS, 2 * SIDE, 1024)
    previous = modes_prev.reshape(2, PAIRS, 2 * SIDE, 1024)
    nbytes = now.size * 4
    wide_shape = jax.ShapeDtypeStruct(now.shape, f32)
    packed_shape = jax.ShapeDtypeStruct((16, PAIRS, SIDE, LANES), f32)
    rows_shape = jax.ShapeDtypeStruct((PAIRS, 3, SIDE, LANES), f32)
    table_shape = jax.ShapeDtypeStruct((PAIRS, 2 * SIDE, LANES), jnp.bfloat16)
    params = pltpu.CompilerParams(vmem_limit_bytes=VMEM_LIMIT)
    wide_scratch = pltpu.VMEM((PAIRS, 2, 2 * SIDE, 1024), f32)
    copied = pltpu.SemaphoreType.DMA((PAIRS,))
    count = lax.axis_size("region")
    upward = [((i + 1) % count, i) for i in range(count)]
    downward = [(i, (i + 1) % count) for i in range(count)]

    with jax.named_scope("plan"):
        y_tables, to_cells, to_modes, masks, places = pl.pallas_call(
            plan_kernel,
            out_shape=(
                jax.ShapeDtypeStruct((PAIRS, 48, LANES), f32),
                table_shape,
                table_shape,
                jax.ShapeDtypeStruct((PAIRS, SIDE, LANES), f32),
                jax.ShapeDtypeStruct((36,), jnp.int32),
            ),
            in_specs=[smem(), smem(), smem()],
            out_specs=(vmem(), vmem(), vmem(), vmem(), smem()),
            compiler_params=params,
            cost_estimate=cost(10**8, 10**6),
        )(extents, partner, offset)

    def encode(part):
        with jax.named_scope("encode"):
            return pl.pallas_call(
                functools.partial(encode_kernel, part),
                out_shape=packed_shape,
                in_specs=[hbm()],
                out_specs=hbm(),
                scratch_shapes=[
                    wide_scratch,
                    pltpu.VMEM((PAIRS, 16, SIDE, LANES), f32),
                    copied,
                    copied,
                ],
                compiler_params=pltpu.CompilerParams(vmem_limit_bytes=ENCODE_LIMIT),
                cost_estimate=cost(10**6, 2 * nbytes),
            )(now)

    def rows_of(held):
        with jax.named_scope("rows"):
            return pl.pallas_call(
                rows_kernel,
                out_shape=rows_shape,
                in_specs=[vmem()] * 3,
                out_specs=vmem(),
                compiler_params=params,
                cost_estimate=cost(10**7, nbytes),
            )(y_tables, to_cells, held)

    def force(rows, up, down):
        with jax.named_scope("force"):
            return pl.pallas_call(
                force_kernel,
                out_shape=packed_shape,
                in_specs=[smem()] + [vmem()] * 6,
                out_specs=vmem(),
                scratch_shapes=[pltpu.VMEM((3 * PAIRS, 3, SIDE, LANES), f32)],
                compiler_params=params,
                cost_estimate=cost(10**7, nbytes),
            )(places, y_tables, to_modes, masks, rows, up, down)

    def exchange(blocks):
        return lax.all_to_all(blocks, "line", 0, 0, tiled=True)

    def halo(rows):
        return lax.ppermute(rows, "region", upward), lax.ppermute(rows, "region", downward)

    sent_one = encode(0)
    held_one = exchange(sent_one)
    sent_two = encode(1)
    held_two = exchange(sent_two)
    rows_one = rows_of(held_one)
    up_one, down_one = halo(rows_one)
    with jax.named_scope("free"):
        base, gain = pl.pallas_call(
            free_kernel,
            out_shape=(wide_shape, wide_shape),
            in_specs=[smem(), hbm(), hbm()],
            out_specs=(hbm(), hbm()),
            scratch_shapes=[pltpu.VMEM(now.shape, f32)] * 4 + [pltpu.SemaphoreType.DMA((2, 4))],
            compiler_params=pltpu.CompilerParams(vmem_limit_bytes=FREE_LIMIT),
            cost_estimate=cost(10**9, 4 * nbytes),
        )(extents, *lax.optimization_barrier((now, previous, rows_one))[:2])
    down_one, base, gain = lax.optimization_barrier((down_one, base, gain))
    mixed_one = exchange(force(rows_one, up_one, down_one))
    rows_two = rows_of(held_two)
    up_two, down_two = halo(rows_two)
    mixed_two = exchange(force(rows_two, up_two, down_two))
    with jax.named_scope("update"):
        result = pl.pallas_call(
            update_kernel,
            out_shape=wide_shape,
            in_specs=[vmem()] * 4,
            out_specs=hbm(),
            scratch_shapes=[wide_scratch, copied],
            compiler_params=params,
            cost_estimate=cost(10**7, 4 * nbytes),
        )(mixed_one, mixed_two, base, gain)
    return result.reshape(modes_now.shape)


def solution(mesh):
    return jax.shard_map(
        shards,
        mesh=mesh,
        in_specs=(P("region", "line", None), P("region", "line", None), P(), P(), P()),
        out_specs=P("region", "line", None),
        check_vma=False,
    )
```

```python
import functools
import math

import jax
import jax.numpy as jnp
from jax import lax
from jax.experimental import pallas as pl
from jax.experimental.pallas import tpu as pltpu
from jax.sharding import PartitionSpec as P

SIDE = 32
PAIRS = 3
OWN = 6
LANES = 128
A1, A2, A3 = 1.5, -0.15, 1.0 / 90.0
VMEM_LIMIT = 16 * 1024 * 1024
ENCODE_LIMIT = 63 * 1024 * 1024
FREE_LIMIT = 52 * 1024 * 1024

SERIES = [2.0 * (-1.0) ** k / math.factorial(2 * k + 2) for k in range(10)]


def series(u, terms):
    total = jnp.full_like(u, SERIES[terms - 1])
    for coefficient in SERIES[: terms - 1][::-1]:
        total = total * u + coefficient
    return total


def cosine_entry(freq, cell, live):
    inverse = 1.0 / live
    turn = 4.0 * live
    steps = freq * (2.0 * cell + 1.0)
    steps = steps - turn * jnp.floor((steps + 0.5) * (0.25 * inverse))
    steps = jnp.minimum(steps, turn - steps)
    flip = steps > live
    steps = jnp.where(flip, 2.0 * live - steps, steps)
    angle = (0.5 * math.pi) * (steps * inverse)
    u = angle * angle
    value = 1.0 - 0.5 * u * series(u, 7)
    value = jnp.where(flip, -value, value)
    weight = jnp.sqrt(jnp.where(freq == 0.0, 1.0, 2.0) * inverse)
    return jnp.where((freq < live) & (cell < live), weight * value, 0.0)


def z_table(live_z, to_cells):
    shape = (SIDE, LANES)
    row = lax.broadcasted_iota(jnp.int32, shape, 0).astype(jnp.float32)
    lane = lax.broadcasted_iota(jnp.int32, shape, 1)
    column = (lane % SIDE).astype(jnp.float32)
    freq, cell = (column, row) if to_cells else (row, column)
    table = cosine_entry(freq, cell, jnp.full(shape, live_z, jnp.float32))
    high = table.astype(jnp.bfloat16).astype(jnp.float32)
    return jnp.where(lane < LANES // 2, high, table - high).astype(jnp.bfloat16)


def z_apply(table, parts):
    values = jnp.concatenate(parts, axis=1)
    high = values.astype(jnp.bfloat16)
    low = (values - high.astype(jnp.float32)).astype(jnp.bfloat16)
    stacked = jnp.concatenate([high, low, high, low], axis=0)
    both = jnp.dot(table, stacked, preferred_element_type=jnp.float32)
    first = even_group((SIDE, LANES))
    return [
        jnp.where(
            first,
            both[:SIDE, i * LANES : (i + 1) * LANES],
            both[SIDE:, i * LANES : (i + 1) * LANES],
        )
        for i in range(len(parts))
    ]


def live(extents, rect, which):
    return extents[which, rect].astype(jnp.float32)


def lanes_of(shape):
    return lax.broadcasted_iota(jnp.int32, shape, len(shape) - 1)


def left_half(shape):
    return lanes_of(shape) < LANES // 2


def even_group(shape):
    return (lanes_of(shape) // SIDE) % 2 == 0


def regroup(tiles, wanted=range(4)):
    group = lanes_of(tiles[0].shape) // SIDE
    at = [group == i for i in range(3)]

    def pick(four):
        return jnp.where(
            at[0], four[0], jnp.where(at[1], four[1], jnp.where(at[2], four[2], four[3]))
        )

    turned = []
    for k in range(4):
        diagonal = pick([tiles[(g + k) % 4] for g in range(4)])
        turned.append(pltpu.roll(diagonal, k * SIDE, 1) if k else diagonal)
    return [pick([turned[(q - g) % 4] for q in range(4)]) for g in wanted]


def encode_kernel(part, now, out, held, made, arrived, sent):
    inward = [
        pltpu.make_async_copy(now.at[:, i], held.at[i], arrived.at[i]) for i in range(PAIRS)
    ]
    outward = [
        pltpu.make_async_copy(made.at[i], out.at[:, i], sent.at[i]) for i in range(PAIRS)
    ]
    for copy in inward:
        copy.start()
    for pair in range(PAIRS):
        inward[pair].wait()
        for chip in range(8):
            lanes = slice(chip * LANES, chip * LANES + LANES)
            tiles = [
                held[pair, h, parity * SIDE : (parity + 1) * SIDE, lanes]
                for parity in range(2)
                for h in range(2)
            ]
            for core, tile in enumerate(regroup(tiles, (part, 2 + part))):
                made[pair, 2 * chip + core] = tile
        outward[pair].start()
    for copy in outward:
        copy.wait()


def plan_kernel(extents, partner, offset, y_tables, to_cells, to_modes, masks, places):
    region = lax.axis_index("region")
    count = lax.axis_size("region")
    first = region * OWN
    total = count * OWN
    shape = (48, LANES)
    index = lax.broadcasted_iota(jnp.int32, shape, 0)
    parity = lanes_of(shape) // (2 * SIDE)
    even = even_group(shape)
    freq = (2 * (index % 16) + parity).astype(jnp.float32)
    cell = (index // 16).astype(jnp.float32)
    for pair in range(PAIRS):
        one, two = first + pair, first + pair + PAIRS
        live_y = jnp.where(even, live(extents, one, 0), live(extents, two, 0))
        y_tables[pair] = cosine_entry(freq, cell, live_y)
        for h, rect in ((0, one), (1, two)):
            live_z = live(extents, rect, 1)
            to_cells[pair, h * SIDE : (h + 1) * SIDE] = z_table(live_z, True)
            to_modes[pair, h * SIDE : (h + 1) * SIDE] = z_table(live_z, False)
    lower_of = [jnp.int32(0)] * OWN
    for w in range(3 * OWN):
        rect = lax.rem(first + total + w - OWN, total)
        target = partner[rect] - first
        for r in range(OWN):
            lower_of[r] = jnp.where(target == r, rect, lower_of[r])
    z = lax.broadcasted_iota(jnp.int32, (SIDE, LANES), 0)
    group = lanes_of((SIDE, LANES)) // SIDE
    for pair in range(PAIRS):
        mask = jnp.zeros((SIDE, LANES), jnp.float32)
        for face in range(2):
            for half in range(2):
                r = pair + PAIRS * half
                rect = first + r
                if face == 1:
                    other = partner[rect]
                    shift = offset[rect]
                else:
                    other = lower_of[r]
                    shift = -offset[other]
                place = lax.div(other, OWN)
                slot = other - place * OWN
                side = lax.div(slot, PAIRS)
                to = 2 * face + half
                at = 3 * (4 * pair + to)
                places[at] = lax.rem(place - region + 1 + count, count) * PAIRS + slot - side * PAIRS
                places[at + 1] = lax.rem(shift + SIDE, SIDE)
                places[at + 2] = lax.rem((to - 2 * (1 - face) - side + 4) * SIDE, LANES)
                source = z - shift
                inside = (source >= 0) & (source < extents[1, other]) & (z < extents[1, rect])
                mask = jnp.where((group == to) & inside, 1.0, mask)
        masks[pair] = mask


def encode_plan_kernel(
    extents, partner, offset, now, out, y_tables, to_cells, to_modes, masks, places, *scratch
):
    encode_kernel(0, now, out, *scratch)
    plan_kernel(extents, partner, offset, y_tables, to_cells, to_modes, masks, places)


def free_kernel(extents, now_hbm, previous_hbm, base_hbm, gain_hbm, now, previous, base, gain, copied):
    inward, outward = [], []
    for h in range(2):
        inward.append(
            (
                pltpu.make_async_copy(now_hbm.at[h], now.at[h], copied.at[h, 0]),
                pltpu.make_async_copy(previous_hbm.at[h], previous.at[h], copied.at[h, 1]),
            )
        )
        outward.append(
            (
                pltpu.make_async_copy(base.at[h], base_hbm.at[h], copied.at[h, 2]),
                pltpu.make_async_copy(gain.at[h], gain_hbm.at[h], copied.at[h, 3]),
            )
        )
        for copy in inward[h]:
            copy.start()
    first = lax.axis_index("region") * OWN
    line = lax.axis_index("line")
    row = lax.broadcasted_iota(jnp.int32, (2 * SIDE, 256), 0)
    freq_y = (2 * line + row // SIDE).astype(jnp.float32)
    freq_z = (row % SIDE).astype(jnp.float32)
    column = lax.broadcasted_iota(jnp.int32, (1, 256), 1)
    quarter = (0.5 * math.pi) ** 2
    for r in range(OWN):
        h, pair = r // PAIRS, r % PAIRS
        if pair == 0:
            for copy in inward[h]:
                copy.wait()
        live_y = live(extents, first + r, 0)
        live_z = live(extents, first + r, 1)
        y = freq_y / live_y
        z = freq_z / live_z
        across = quarter * (y * y + z * z)
        active = (freq_y < live_y) & (freq_z < live_z)
        for chunk in range(4):
            lanes = slice(chunk * 256, chunk * 256 + 256)
            x = (column + chunk * 256).astype(jnp.float32) * (1.0 / 1024.0)
            u = across + quarter * (x * x)
            s = series(u, 9)
            stepped = (2.0 - u * s) * now[h, pair, :, lanes] - previous[h, pair, :, lanes]
            base[h, pair, :, lanes] = jnp.where(active, stepped, 0.0)
            gain[h, pair, :, lanes] = jnp.where(active, 0.25 * s, 0.0)
        if pair == PAIRS - 1:
            for copy in outward[h]:
                copy.start()
    for copies in outward:
        for copy in copies:
            copy.wait()


def fold(packed):
    swapped = pltpu.roll(packed, LANES // 2, 1)
    return jnp.where(left_half(packed.shape), packed + swapped, swapped - packed)


def rows_kernel(tables, to_cells, modes, rows):
    for pair in range(PAIRS):
        totals = [None] * 3
        for source in range(16):
            block = modes[source, pair]
            for e in range(3):
                at = e * 16 + source
                term = tables[pair, at : at + 1] * block
                totals[e] = term if totals[e] is None else totals[e] + term
        for e, cells in enumerate(z_apply(to_cells[pair], [fold(t) for t in totals])):
            rows[pair, e] = cells


def spread(d):
    return [A1 * d[0] + A2 * d[1] + A3 * d[2], A2 * d[0] + A3 * d[1], A3 * d[0]]


def force_kernel(places, tables, to_modes, masks, own, up, down, out, near):
    for pair in range(PAIRS):
        near[pair] = down[pair]
        near[PAIRS + pair] = own[pair]
        near[2 * PAIRS + pair] = up[pair]
    group = lanes_of((3, SIDE, LANES)) // SIDE
    for pair in range(PAIRS):
        both = None
        for to in range(4):
            at = 3 * (4 * pair + to)
            cells = pltpu.roll(near[places[at]], places[at + 1], 1)
            cells = pltpu.roll(cells, places[at + 2], 2)
            both = cells if both is None else jnp.where(group == to, cells, both)
        mask = masks[pair]
        parts = spread([mask * (both[e] - own[pair, e]) for e in range(3)])
        parts = z_apply(to_modes[pair], [fold(part) for part in parts])
        for target in range(16):
            value = None
            for e in range(3):
                at = e * 16 + target
                term = tables[pair, at : at + 1] * parts[e]
                value = term if value is None else value + term
            out[target, pair] = value


def update_kernel(mixed_one, mixed_two, base, gain, out, made, sent):
    copies = []
    for pair in range(PAIRS):
        for chip in range(8):
            lanes = slice(chip * LANES, chip * LANES + LANES)
            tiles = regroup(
                [mixed[2 * chip + core, pair] for core in range(2) for mixed in (mixed_one, mixed_two)]
            )
            for parity in range(2):
                modes = slice(parity * SIDE, parity * SIDE + SIDE)
                for h in range(2):
                    made[pair, h, modes, lanes] = (
                        base[h, pair, modes, lanes]
                        + gain[h, pair, modes, lanes] * tiles[2 * parity + h]
                    )
        copies.append(pltpu.make_async_copy(made.at[pair], out.at[:, pair], sent.at[pair]))
        copies[-1].start()
    for copy in copies:
        copy.wait()


def smem():
    return pl.BlockSpec(memory_space=pltpu.SMEM)


def vmem():
    return pl.BlockSpec(memory_space=pltpu.VMEM)


def hbm():
    return pl.BlockSpec(memory_space=pltpu.HBM)


def cost(flops, nbytes):
    return pl.CostEstimate(flops=flops, bytes_accessed=nbytes, transcendentals=0)


def shards(modes_now, modes_prev, extents, partner, offset):
    f32 = jnp.float32
    extents = extents.T
    now = modes_now.reshape(2, PAIRS, 2 * SIDE, 1024)
    previous = modes_prev.reshape(2, PAIRS, 2 * SIDE, 1024)
    nbytes = now.size * 4
    wide_shape = jax.ShapeDtypeStruct(now.shape, f32)
    packed_shape = jax.ShapeDtypeStruct((16, PAIRS, SIDE, LANES), f32)
    rows_shape = jax.ShapeDtypeStruct((PAIRS, 3, SIDE, LANES), f32)
    table_shape = jax.ShapeDtypeStruct((PAIRS, 2 * SIDE, LANES), jnp.bfloat16)
    params = pltpu.CompilerParams(vmem_limit_bytes=VMEM_LIMIT)
    wide_scratch = pltpu.VMEM((PAIRS, 2, 2 * SIDE, 1024), f32)
    copied = pltpu.SemaphoreType.DMA((PAIRS,))
    count = lax.axis_size("region")
    upward = [((i + 1) % count, i) for i in range(count)]
    downward = [(i, (i + 1) % count) for i in range(count)]

    encode_scratch = [
        wide_scratch,
        pltpu.VMEM((PAIRS, 16, SIDE, LANES), f32),
        copied,
        copied,
    ]
    encode_params = pltpu.CompilerParams(vmem_limit_bytes=ENCODE_LIMIT)
    with jax.named_scope("encode"):
        sent_two = pl.pallas_call(
            functools.partial(encode_kernel, 1),
            out_shape=packed_shape,
            in_specs=[hbm()],
            out_specs=hbm(),
            scratch_shapes=encode_scratch,
            compiler_params=encode_params,
            cost_estimate=cost(10**6, 2 * nbytes),
        )(now)
    with jax.named_scope("encode_plan"):
        sent_one, y_tables, to_cells, to_modes, masks, places = pl.pallas_call(
            encode_plan_kernel,
            out_shape=(
                packed_shape,
                jax.ShapeDtypeStruct((PAIRS, 48, LANES), f32),
                table_shape,
                table_shape,
                jax.ShapeDtypeStruct((PAIRS, SIDE, LANES), f32),
                jax.ShapeDtypeStruct((36,), jnp.int32),
            ),
            in_specs=[smem(), smem(), smem(), hbm()],
            out_specs=(hbm(), vmem(), vmem(), vmem(), vmem(), smem()),
            scratch_shapes=encode_scratch,
            compiler_params=encode_params,
            cost_estimate=cost(10**6, 2 * nbytes),
        )(extents, partner, offset, lax.optimization_barrier((now, sent_two))[0])

    def rows_of(held):
        with jax.named_scope("rows"):
            return pl.pallas_call(
                rows_kernel,
                out_shape=rows_shape,
                in_specs=[vmem()] * 3,
                out_specs=vmem(),
                compiler_params=params,
                cost_estimate=cost(10**7, nbytes),
            )(y_tables, to_cells, held)

    def force(rows, up, down):
        with jax.named_scope("force"):
            return pl.pallas_call(
                force_kernel,
                out_shape=packed_shape,
                in_specs=[smem()] + [vmem()] * 6,
                out_specs=vmem(),
                scratch_shapes=[pltpu.VMEM((3 * PAIRS, 3, SIDE, LANES), f32)],
                compiler_params=params,
                cost_estimate=cost(10**7, nbytes),
            )(places, y_tables, to_modes, masks, rows, up, down)

    def exchange(blocks):
        return lax.all_to_all(blocks, "line", 0, 0, tiled=True)

    def halo(rows):
        return lax.ppermute(rows, "region", upward), lax.ppermute(rows, "region", downward)

    held_one = exchange(sent_one)
    held_two = exchange(sent_two)
    rows_one = rows_of(held_one)
    up_one, down_one = halo(rows_one)
    with jax.named_scope("free"):
        base, gain = pl.pallas_call(
            free_kernel,
            out_shape=(wide_shape, wide_shape),
            in_specs=[smem(), hbm(), hbm()],
            out_specs=(hbm(), hbm()),
            scratch_shapes=[pltpu.VMEM(now.shape, f32)] * 4 + [pltpu.SemaphoreType.DMA((2, 4))],
            compiler_params=pltpu.CompilerParams(vmem_limit_bytes=FREE_LIMIT),
            cost_estimate=cost(10**9, 4 * nbytes),
        )(extents, *lax.optimization_barrier((now, previous, rows_one))[:2])
    down_one, base, gain = lax.optimization_barrier((down_one, base, gain))
    mixed_one = exchange(force(rows_one, up_one, down_one))
    rows_two = rows_of(held_two)
    up_two, down_two = halo(rows_two)
    mixed_two = exchange(force(rows_two, up_two, down_two))
    with jax.named_scope("update"):
        result = pl.pallas_call(
            update_kernel,
            out_shape=wide_shape,
            in_specs=[vmem()] * 4,
            out_specs=hbm(),
            scratch_shapes=[wide_scratch, copied],
            compiler_params=params,
            cost_estimate=cost(10**7, 4 * nbytes),
        )(mixed_one, mixed_two, base, gain)
    return result.reshape(modes_now.shape)


def solution(mesh):
    return jax.shard_map(
        shards,
        mesh=mesh,
        in_specs=(P("region", "line", None), P("region", "line", None), P(), P(), P()),
        out_specs=P("region", "line", None),
        check_vma=False,
    )
```

```python
import functools
import math

import jax
import jax.numpy as jnp
from jax import lax
from jax.experimental import pallas as pl
from jax.experimental.pallas import tpu as pltpu
from jax.sharding import PartitionSpec as P

SIDE = 32
PAIRS = 3
OWN = 6
LANES = 128
A1, A2, A3 = 1.5, -0.15, 1.0 / 90.0
VMEM_LIMIT = 16 * 1024 * 1024
ENCODE_LIMIT = 63 * 1024 * 1024
FREE_LIMIT = 52 * 1024 * 1024

SERIES = [2.0 * (-1.0) ** k / math.factorial(2 * k + 2) for k in range(10)]


def series(u, terms):
    total = jnp.full_like(u, SERIES[terms - 1])
    for coefficient in SERIES[: terms - 1][::-1]:
        total = total * u + coefficient
    return total


def cosine_entry(freq, cell, live):
    inverse = 1.0 / live
    turn = 4.0 * live
    steps = freq * (2.0 * cell + 1.0)
    steps = steps - turn * jnp.floor((steps + 0.5) * (0.25 * inverse))
    steps = jnp.minimum(steps, turn - steps)
    flip = steps > live
    steps = jnp.where(flip, 2.0 * live - steps, steps)
    angle = (0.5 * math.pi) * (steps * inverse)
    u = angle * angle
    value = 1.0 - 0.5 * u * series(u, 7)
    value = jnp.where(flip, -value, value)
    weight = jnp.sqrt(jnp.where(freq == 0.0, 1.0, 2.0) * inverse)
    return jnp.where((freq < live) & (cell < live), weight * value, 0.0)


def z_table(live_z, to_cells):
    shape = (SIDE, LANES)
    row = lax.broadcasted_iota(jnp.int32, shape, 0).astype(jnp.float32)
    lane = lax.broadcasted_iota(jnp.int32, shape, 1)
    column = (lane % SIDE).astype(jnp.float32)
    freq, cell = (column, row) if to_cells else (row, column)
    table = cosine_entry(freq, cell, jnp.full(shape, live_z, jnp.float32))
    high = table.astype(jnp.bfloat16).astype(jnp.float32)
    return jnp.where(lane < LANES // 2, high, table - high).astype(jnp.bfloat16)


def z_apply(table, parts):
    values = jnp.concatenate(parts, axis=1)
    high = values.astype(jnp.bfloat16)
    low = (values - high.astype(jnp.float32)).astype(jnp.bfloat16)
    stacked = jnp.concatenate([high, low, high, low], axis=0)
    both = jnp.dot(table, stacked, preferred_element_type=jnp.float32)
    first = even_group((SIDE, LANES))
    return [
        jnp.where(
            first,
            both[:SIDE, i * LANES : (i + 1) * LANES],
            both[SIDE:, i * LANES : (i + 1) * LANES],
        )
        for i in range(len(parts))
    ]


def live(extents, rect, which):
    return extents[which, rect].astype(jnp.float32)


def lanes_of(shape):
    return lax.broadcasted_iota(jnp.int32, shape, len(shape) - 1)


def left_half(shape):
    return lanes_of(shape) < LANES // 2


def even_group(shape):
    return (lanes_of(shape) // SIDE) % 2 == 0


def regroup(tiles, wanted=range(4)):
    group = lanes_of(tiles[0].shape) // SIDE
    at = [group == i for i in range(3)]

    def pick(four):
        return jnp.where(
            at[0], four[0], jnp.where(at[1], four[1], jnp.where(at[2], four[2], four[3]))
        )

    turned = []
    for k in range(4):
        diagonal = pick([tiles[(g + k) % 4] for g in range(4)])
        turned.append(pltpu.roll(diagonal, k * SIDE, 1) if k else diagonal)
    return [pick([turned[(q - g) % 4] for q in range(4)]) for g in wanted]


def encode_kernel(part, now, out, held, made, arrived, sent):
    inward = [
        pltpu.make_async_copy(now.at[:, i], held.at[i], arrived.at[i]) for i in range(PAIRS)
    ]
    outward = [
        pltpu.make_async_copy(made.at[i], out.at[:, i], sent.at[i]) for i in range(PAIRS)
    ]
    for copy in inward:
        copy.start()
    for pair in range(PAIRS):
        inward[pair].wait()
        for chip in range(8):
            lanes = slice(chip * LANES, chip * LANES + LANES)
            tiles = [
                held[pair, h, parity * SIDE : (parity + 1) * SIDE, lanes]
                for parity in range(2)
                for h in range(2)
            ]
            for core, tile in enumerate(regroup(tiles, (part, 2 + part))):
                made[pair, 2 * chip + core] = tile
        outward[pair].start()
    for copy in outward:
        copy.wait()


def plan_kernel(extents, partner, offset, y_tables, to_cells, to_modes, masks, places):
    region = lax.axis_index("region")
    count = lax.axis_size("region")
    first = region * OWN
    total = count * OWN
    shape = (48, LANES)
    index = lax.broadcasted_iota(jnp.int32, shape, 0)
    parity = lanes_of(shape) // (2 * SIDE)
    even = even_group(shape)
    freq = (2 * (index % 16) + parity).astype(jnp.float32)
    cell = (index // 16).astype(jnp.float32)
    for pair in range(PAIRS):
        one, two = first + pair, first + pair + PAIRS
        live_y = jnp.where(even, live(extents, one, 0), live(extents, two, 0))
        y_tables[pair] = cosine_entry(freq, cell, live_y)
        for h, rect in ((0, one), (1, two)):
            live_z = live(extents, rect, 1)
            to_cells[pair, h * SIDE : (h + 1) * SIDE] = z_table(live_z, True)
            to_modes[pair, h * SIDE : (h + 1) * SIDE] = z_table(live_z, False)
    lower_of = [jnp.int32(0)] * OWN
    for w in range(3 * OWN):
        rect = lax.rem(first + total + w - OWN, total)
        target = partner[rect] - first
        for r in range(OWN):
            lower_of[r] = jnp.where(target == r, rect, lower_of[r])
    z = lax.broadcasted_iota(jnp.int32, (SIDE, LANES), 0)
    group = lanes_of((SIDE, LANES)) // SIDE
    for pair in range(PAIRS):
        mask = jnp.zeros((SIDE, LANES), jnp.float32)
        for face in range(2):
            for half in range(2):
                r = pair + PAIRS * half
                rect = first + r
                if face == 1:
                    other = partner[rect]
                    shift = offset[rect]
                else:
                    other = lower_of[r]
                    shift = -offset[other]
                place = lax.div(other, OWN)
                slot = other - place * OWN
                side = lax.div(slot, PAIRS)
                to = 2 * face + half
                at = 3 * (4 * pair + to)
                places[at] = lax.rem(place - region + 1 + count, count) * PAIRS + slot - side * PAIRS
                places[at + 1] = lax.rem(shift + SIDE, SIDE)
                places[at + 2] = lax.rem((to - 2 * (1 - face) - side + 4) * SIDE, LANES)
                source = z - shift
                inside = (source >= 0) & (source < extents[1, other]) & (z < extents[1, rect])
                mask = jnp.where((group == to) & inside, 1.0, mask)
        masks[pair] = mask


def encode_plan_kernel(
    extents, partner, offset, now, out, y_tables, to_cells, to_modes, masks, places, *scratch
):
    encode_kernel(0, now, out, *scratch)
    plan_kernel(extents, partner, offset, y_tables, to_cells, to_modes, masks, places)


def free_kernel(extents, now_hbm, previous_hbm, base_hbm, gain_hbm, now, previous, base, gain, copied):
    inward, outward = [], []
    for r in range(OWN):
        h, pair = r // PAIRS, r % PAIRS
        ends = (
            (now_hbm.at[h, pair], now.at[h, pair]),
            (previous_hbm.at[h, pair], previous.at[h, pair]),
            (base.at[h, pair], base_hbm.at[h, pair]),
            (gain.at[h, pair], gain_hbm.at[h, pair]),
        )
        copies = [pltpu.make_async_copy(*ends[i], copied.at[r, i]) for i in range(4)]
        inward.append(copies[:2])
        outward.append(copies[2:])
        for copy in inward[r]:
            copy.start()
    first = lax.axis_index("region") * OWN
    line = lax.axis_index("line")
    row = lax.broadcasted_iota(jnp.int32, (2 * SIDE, 256), 0)
    freq_y = (2 * line + row // SIDE).astype(jnp.float32)
    freq_z = (row % SIDE).astype(jnp.float32)
    column = lax.broadcasted_iota(jnp.int32, (1, 256), 1)
    quarter = (0.5 * math.pi) ** 2
    for r in range(OWN):
        h, pair = r // PAIRS, r % PAIRS
        for copy in inward[r]:
            copy.wait()
        live_y = live(extents, first + r, 0)
        live_z = live(extents, first + r, 1)
        y = freq_y / live_y
        z = freq_z / live_z
        across = quarter * (y * y + z * z)
        active = (freq_y < live_y) & (freq_z < live_z)
        for chunk in range(4):
            lanes = slice(chunk * 256, chunk * 256 + 256)
            x = (column + chunk * 256).astype(jnp.float32) * (1.0 / 1024.0)
            u = across + quarter * (x * x)
            s = series(u, 9)
            stepped = (2.0 - u * s) * now[h, pair, :, lanes] - previous[h, pair, :, lanes]
            base[h, pair, :, lanes] = jnp.where(active, stepped, 0.0)
            gain[h, pair, :, lanes] = jnp.where(active, 0.25 * s, 0.0)
        for copy in outward[r]:
            copy.start()
    for copies in outward:
        for copy in copies:
            copy.wait()


def fold(packed):
    swapped = pltpu.roll(packed, LANES // 2, 1)
    return jnp.where(left_half(packed.shape), packed + swapped, swapped - packed)


def rows_kernel(tables, to_cells, modes, rows):
    for pair in range(PAIRS):
        totals = [None] * 3
        for source in range(16):
            block = modes[source, pair]
            for e in range(3):
                at = e * 16 + source
                term = tables[pair, at : at + 1] * block
                totals[e] = term if totals[e] is None else totals[e] + term
        for e, cells in enumerate(z_apply(to_cells[pair], [fold(t) for t in totals])):
            rows[pair, e] = cells


def spread(d):
    return [A1 * d[0] + A2 * d[1] + A3 * d[2], A2 * d[0] + A3 * d[1], A3 * d[0]]


def force_kernel(places, tables, to_modes, masks, own, up, down, out, near):
    for pair in range(PAIRS):
        near[pair] = down[pair]
        near[PAIRS + pair] = own[pair]
        near[2 * PAIRS + pair] = up[pair]
    group = lanes_of((3, SIDE, LANES)) // SIDE
    for pair in range(PAIRS):
        both = None
        for to in range(4):
            at = 3 * (4 * pair + to)
            cells = pltpu.roll(near[places[at]], places[at + 1], 1)
            cells = pltpu.roll(cells, places[at + 2], 2)
            both = cells if both is None else jnp.where(group == to, cells, both)
        mask = masks[pair]
        parts = spread([mask * (both[e] - own[pair, e]) for e in range(3)])
        parts = z_apply(to_modes[pair], [fold(part) for part in parts])
        for target in range(16):
            value = None
            for e in range(3):
                at = e * 16 + target
                term = tables[pair, at : at + 1] * parts[e]
                value = term if value is None else value + term
            out[target, pair] = value


def update_kernel(mixed_one, mixed_two, base, gain, out, made, sent):
    copies = []
    for pair in range(PAIRS):
        for chip in range(8):
            lanes = slice(chip * LANES, chip * LANES + LANES)
            tiles = regroup(
                [mixed[2 * chip + core, pair] for core in range(2) for mixed in (mixed_one, mixed_two)]
            )
            for parity in range(2):
                modes = slice(parity * SIDE, parity * SIDE + SIDE)
                for h in range(2):
                    made[pair, h, modes, lanes] = (
                        base[h, pair, modes, lanes]
                        + gain[h, pair, modes, lanes] * tiles[2 * parity + h]
                    )
        copies.append(pltpu.make_async_copy(made.at[pair], out.at[:, pair], sent.at[pair]))
        copies[-1].start()
    for copy in copies:
        copy.wait()


def smem():
    return pl.BlockSpec(memory_space=pltpu.SMEM)


def vmem():
    return pl.BlockSpec(memory_space=pltpu.VMEM)


def hbm():
    return pl.BlockSpec(memory_space=pltpu.HBM)


def cost(flops, nbytes):
    return pl.CostEstimate(flops=flops, bytes_accessed=nbytes, transcendentals=0)


def shards(modes_now, modes_prev, extents, partner, offset):
    f32 = jnp.float32
    extents = extents.T
    now = modes_now.reshape(2, PAIRS, 2 * SIDE, 1024)
    previous = modes_prev.reshape(2, PAIRS, 2 * SIDE, 1024)
    nbytes = now.size * 4
    wide_shape = jax.ShapeDtypeStruct(now.shape, f32)
    packed_shape = jax.ShapeDtypeStruct((16, PAIRS, SIDE, LANES), f32)
    rows_shape = jax.ShapeDtypeStruct((PAIRS, 3, SIDE, LANES), f32)
    table_shape = jax.ShapeDtypeStruct((PAIRS, 2 * SIDE, LANES), jnp.bfloat16)
    params = pltpu.CompilerParams(vmem_limit_bytes=VMEM_LIMIT)
    wide_scratch = pltpu.VMEM((PAIRS, 2, 2 * SIDE, 1024), f32)
    copied = pltpu.SemaphoreType.DMA((PAIRS,))
    count = lax.axis_size("region")
    upward = [((i + 1) % count, i) for i in range(count)]
    downward = [(i, (i + 1) % count) for i in range(count)]

    encode_scratch = [
        wide_scratch,
        pltpu.VMEM((PAIRS, 16, SIDE, LANES), f32),
        copied,
        copied,
    ]
    encode_params = pltpu.CompilerParams(vmem_limit_bytes=ENCODE_LIMIT)
    with jax.named_scope("encode"):
        sent_two = pl.pallas_call(
            functools.partial(encode_kernel, 1),
            out_shape=packed_shape,
            in_specs=[hbm()],
            out_specs=hbm(),
            scratch_shapes=encode_scratch,
            compiler_params=encode_params,
            cost_estimate=cost(10**6, 2 * nbytes),
        )(now)
    with jax.named_scope("encode_plan"):
        sent_one, y_tables, to_cells, to_modes, masks, places = pl.pallas_call(
            encode_plan_kernel,
            out_shape=(
                packed_shape,
                jax.ShapeDtypeStruct((PAIRS, 48, LANES), f32),
                table_shape,
                table_shape,
                jax.ShapeDtypeStruct((PAIRS, SIDE, LANES), f32),
                jax.ShapeDtypeStruct((36,), jnp.int32),
            ),
            in_specs=[smem(), smem(), smem(), hbm()],
            out_specs=(hbm(), vmem(), vmem(), vmem(), vmem(), smem()),
            scratch_shapes=encode_scratch,
            compiler_params=encode_params,
            cost_estimate=cost(10**6, 2 * nbytes),
        )(extents, partner, offset, lax.optimization_barrier((now, sent_two))[0])

    def rows_of(held):
        with jax.named_scope("rows"):
            return pl.pallas_call(
                rows_kernel,
                out_shape=rows_shape,
                in_specs=[vmem()] * 3,
                out_specs=vmem(),
                compiler_params=params,
                cost_estimate=cost(10**7, nbytes),
            )(y_tables, to_cells, held)

    def force(rows, up, down):
        with jax.named_scope("force"):
            return pl.pallas_call(
                force_kernel,
                out_shape=packed_shape,
                in_specs=[smem()] + [vmem()] * 6,
                out_specs=vmem(),
                scratch_shapes=[pltpu.VMEM((3 * PAIRS, 3, SIDE, LANES), f32)],
                compiler_params=params,
                cost_estimate=cost(10**7, nbytes),
            )(places, y_tables, to_modes, masks, rows, up, down)

    def exchange(blocks):
        return lax.all_to_all(blocks, "line", 0, 0, tiled=True)

    def halo(rows):
        return lax.ppermute(rows, "region", upward), lax.ppermute(rows, "region", downward)

    held_one = exchange(sent_one)
    held_two = exchange(sent_two)
    rows_one = rows_of(held_one)
    up_one, down_one = halo(rows_one)
    with jax.named_scope("free"):
        base, gain = pl.pallas_call(
            free_kernel,
            out_shape=(wide_shape, wide_shape),
            in_specs=[smem(), hbm(), hbm()],
            out_specs=(hbm(), hbm()),
            scratch_shapes=[pltpu.VMEM(now.shape, f32)] * 4 + [pltpu.SemaphoreType.DMA((OWN, 4))],
            compiler_params=pltpu.CompilerParams(vmem_limit_bytes=FREE_LIMIT),
            cost_estimate=cost(10**9, 4 * nbytes),
        )(extents, *lax.optimization_barrier((now, previous, rows_one))[:2])
    down_one, base, gain = lax.optimization_barrier((down_one, base, gain))
    mixed_one = exchange(force(rows_one, up_one, down_one))
    rows_two = rows_of(held_two)
    up_two, down_two = halo(rows_two)
    mixed_two = exchange(force(rows_two, up_two, down_two))
    with jax.named_scope("update"):
        result = pl.pallas_call(
            update_kernel,
            out_shape=wide_shape,
            in_specs=[vmem()] * 4,
            out_specs=hbm(),
            scratch_shapes=[wide_scratch, copied],
            compiler_params=params,
            cost_estimate=cost(10**7, 4 * nbytes),
        )(mixed_one, mixed_two, base, gain)
    return result.reshape(modes_now.shape)


def solution(mesh):
    return jax.shard_map(
        shards,
        mesh=mesh,
        in_specs=(P("region", "line", None), P("region", "line", None), P(), P(), P()),
        out_specs=P("region", "line", None),
        check_vma=False,
    )
```

```python
import functools
import math

import jax
import jax.numpy as jnp
from jax import lax
from jax.experimental import pallas as pl
from jax.experimental.pallas import tpu as pltpu
from jax.sharding import PartitionSpec as P

SIDE = 32
PAIRS = 3
OWN = 6
LANES = 128
A1, A2, A3 = 1.5, -0.15, 1.0 / 90.0
VMEM_LIMIT = 16 * 1024 * 1024
ENCODE_LIMIT = 63 * 1024 * 1024
FREE_LIMIT = 52 * 1024 * 1024

SERIES = [2.0 * (-1.0) ** k / math.factorial(2 * k + 2) for k in range(10)]


def series(u, terms):
    total = jnp.full_like(u, SERIES[terms - 1])
    for coefficient in SERIES[: terms - 1][::-1]:
        total = total * u + coefficient
    return total


def cosine_entry(freq, cell, live):
    inverse = 1.0 / live
    turn = 4.0 * live
    steps = freq * (2.0 * cell + 1.0)
    steps = steps - turn * jnp.floor((steps + 0.5) * (0.25 * inverse))
    steps = jnp.minimum(steps, turn - steps)
    flip = steps > live
    steps = jnp.where(flip, 2.0 * live - steps, steps)
    angle = (0.5 * math.pi) * (steps * inverse)
    u = angle * angle
    value = 1.0 - 0.5 * u * series(u, 7)
    value = jnp.where(flip, -value, value)
    weight = jnp.sqrt(jnp.where(freq == 0.0, 1.0, 2.0) * inverse)
    return jnp.where((freq < live) & (cell < live), weight * value, 0.0)


def z_table(live_z, to_cells):
    shape = (SIDE, LANES)
    row = lax.broadcasted_iota(jnp.int32, shape, 0).astype(jnp.float32)
    lane = lax.broadcasted_iota(jnp.int32, shape, 1)
    column = (lane % SIDE).astype(jnp.float32)
    freq, cell = (column, row) if to_cells else (row, column)
    table = cosine_entry(freq, cell, jnp.full(shape, live_z, jnp.float32))
    high = table.astype(jnp.bfloat16).astype(jnp.float32)
    return jnp.where(lane < LANES // 2, high, table - high).astype(jnp.bfloat16)


def z_apply(table, parts):
    values = jnp.concatenate(parts, axis=1)
    high = values.astype(jnp.bfloat16)
    low = (values - high.astype(jnp.float32)).astype(jnp.bfloat16)
    stacked = jnp.concatenate([high, low, high, low], axis=0)
    both = jnp.dot(table, stacked, preferred_element_type=jnp.float32)
    first = even_group((SIDE, LANES))
    return [
        jnp.where(
            first,
            both[:SIDE, i * LANES : (i + 1) * LANES],
            both[SIDE:, i * LANES : (i + 1) * LANES],
        )
        for i in range(len(parts))
    ]


def live(extents, rect, which):
    return extents[which, rect].astype(jnp.float32)


def lanes_of(shape):
    return lax.broadcasted_iota(jnp.int32, shape, len(shape) - 1)


def left_half(shape):
    return lanes_of(shape) < LANES // 2


def even_group(shape):
    return (lanes_of(shape) // SIDE) % 2 == 0


def regroup(tiles, wanted=range(4)):
    group = lanes_of(tiles[0].shape) // SIDE
    at = [group == i for i in range(3)]

    def pick(four):
        return jnp.where(
            at[0], four[0], jnp.where(at[1], four[1], jnp.where(at[2], four[2], four[3]))
        )

    turned = []
    for k in range(4):
        diagonal = pick([tiles[(g + k) % 4] for g in range(4)])
        turned.append(pltpu.roll(diagonal, k * SIDE, 1) if k else diagonal)
    return [pick([turned[(q - g) % 4] for q in range(4)]) for g in wanted]


def encode_kernel(part, now, out, held, made, arrived, sent):
    inward = [
        pltpu.make_async_copy(now.at[:, i], held.at[i], arrived.at[i]) for i in range(PAIRS)
    ]
    outward = [
        pltpu.make_async_copy(made.at[i], out.at[:, i], sent.at[i]) for i in range(PAIRS)
    ]
    for copy in inward:
        copy.start()
    for pair in range(PAIRS):
        inward[pair].wait()
        for chip in range(8):
            lanes = slice(chip * LANES, chip * LANES + LANES)
            tiles = [
                held[pair, h, parity * SIDE : (parity + 1) * SIDE, lanes]
                for parity in range(2)
                for h in range(2)
            ]
            for core, tile in enumerate(regroup(tiles, (part, 2 + part))):
                made[pair, 2 * chip + core] = tile
        outward[pair].start()
    for copy in outward:
        copy.wait()


def plan_kernel(extents, partner, offset, y_tables, to_cells, to_modes, masks, places):
    region = lax.axis_index("region")
    count = lax.axis_size("region")
    first = region * OWN
    total = count * OWN
    shape = (48, LANES)
    index = lax.broadcasted_iota(jnp.int32, shape, 0)
    parity = lanes_of(shape) // (2 * SIDE)
    even = even_group(shape)
    freq = (2 * (index % 16) + parity).astype(jnp.float32)
    cell = (index // 16).astype(jnp.float32)
    for pair in range(PAIRS):
        one, two = first + pair, first + pair + PAIRS
        live_y = jnp.where(even, live(extents, one, 0), live(extents, two, 0))
        y_tables[pair] = cosine_entry(freq, cell, live_y)
        for h, rect in ((0, one), (1, two)):
            live_z = live(extents, rect, 1)
            to_cells[pair, h * SIDE : (h + 1) * SIDE] = z_table(live_z, True)
            to_modes[pair, h * SIDE : (h + 1) * SIDE] = z_table(live_z, False)
    lower_of = [jnp.int32(0)] * OWN
    for w in range(3 * OWN):
        rect = lax.rem(first + total + w - OWN, total)
        target = partner[rect] - first
        for r in range(OWN):
            lower_of[r] = jnp.where(target == r, rect, lower_of[r])
    z = lax.broadcasted_iota(jnp.int32, (SIDE, LANES), 0)
    group = lanes_of((SIDE, LANES)) // SIDE
    for pair in range(PAIRS):
        mask = jnp.zeros((SIDE, LANES), jnp.float32)
        for face in range(2):
            for half in range(2):
                r = pair + PAIRS * half
                rect = first + r
                if face == 1:
                    other = partner[rect]
                    shift = offset[rect]
                else:
                    other = lower_of[r]
                    shift = -offset[other]
                place = lax.div(other, OWN)
                slot = other - place * OWN
                side = lax.div(slot, PAIRS)
                to = 2 * face + half
                at = 3 * (4 * pair + to)
                places[at] = lax.rem(place - region + 1 + count, count) * PAIRS + slot - side * PAIRS
                places[at + 1] = lax.rem(shift + SIDE, SIDE)
                places[at + 2] = lax.rem((to - 2 * (1 - face) - side + 4) * SIDE, LANES)
                source = z - shift
                inside = (source >= 0) & (source < extents[1, other]) & (z < extents[1, rect])
                mask = jnp.where((group == to) & inside, 1.0, mask)
        masks[pair] = mask


def encode_plan_kernel(
    extents, partner, offset, now, out, y_tables, to_cells, to_modes, masks, places, *scratch
):
    encode_kernel(0, now, out, *scratch)
    plan_kernel(extents, partner, offset, y_tables, to_cells, to_modes, masks, places)


def free_kernel(extents, now_hbm, previous_hbm, base_hbm, gain_hbm, now, previous, base, gain, copied):
    inward, outward = [], []
    for r in range(OWN):
        h, pair = r // PAIRS, r % PAIRS
        ends = (
            (now_hbm.at[h, pair], now.at[h, pair]),
            (previous_hbm.at[h, pair], previous.at[h, pair]),
            (base.at[h, pair], base_hbm.at[h, pair]),
            (gain.at[h, pair], gain_hbm.at[h, pair]),
        )
        copies = [pltpu.make_async_copy(*ends[i], copied.at[r, i]) for i in range(4)]
        inward.append(copies[:2])
        outward.append(copies[2:])
        for copy in inward[r]:
            copy.start()
    first = lax.axis_index("region") * OWN
    line = lax.axis_index("line")
    row = lax.broadcasted_iota(jnp.int32, (2 * SIDE, 256), 0)
    freq_y = (2 * line + row // SIDE).astype(jnp.float32)
    freq_z = (row % SIDE).astype(jnp.float32)
    column = lax.broadcasted_iota(jnp.int32, (1, 256), 1)
    quarter = (0.5 * math.pi) ** 2
    for r in range(OWN):
        h, pair = r // PAIRS, r % PAIRS
        for copy in inward[r]:
            copy.wait()
        live_y = live(extents, first + r, 0)
        live_z = live(extents, first + r, 1)
        y = freq_y / live_y
        z = freq_z / live_z
        across = quarter * (y * y + z * z)
        active = (freq_y < live_y) & (freq_z < live_z)
        for chunk in range(4):
            lanes = slice(chunk * 256, chunk * 256 + 256)
            x = (column + chunk * 256).astype(jnp.float32) * (1.0 / 1024.0)
            u = across + quarter * (x * x)
            s = series(u, 9)
            stepped = (2.0 - u * s) * now[h, pair, :, lanes] - previous[h, pair, :, lanes]
            base[h, pair, :, lanes] = jnp.where(active, stepped, 0.0)
            gain[h, pair, :, lanes] = jnp.where(active, 0.25 * s, 0.0)
        for copy in outward[r]:
            copy.start()
    for copies in outward:
        for copy in copies:
            copy.wait()


def fold(packed):
    swapped = pltpu.roll(packed, LANES // 2, 1)
    return jnp.where(left_half(packed.shape), packed + swapped, swapped - packed)


def rows_kernel(tables, to_cells, modes, rows):
    for pair in range(PAIRS):
        totals = [None] * 3
        for source in range(16):
            block = modes[source, pair]
            for e in range(3):
                at = e * 16 + source
                term = tables[pair, at : at + 1] * block
                totals[e] = term if totals[e] is None else totals[e] + term
        for e, cells in enumerate(z_apply(to_cells[pair], [fold(t) for t in totals])):
            rows[pair, e] = cells


def spread(d):
    return [A1 * d[0] + A2 * d[1] + A3 * d[2], A2 * d[0] + A3 * d[1], A3 * d[0]]


def force_kernel(places, tables, to_modes, masks, own, up, down, out, near):
    for pair in range(PAIRS):
        near[pair] = down[pair]
        near[PAIRS + pair] = own[pair]
        near[2 * PAIRS + pair] = up[pair]
    group = lanes_of((3, SIDE, LANES)) // SIDE
    for pair in range(PAIRS):
        both = None
        for to in range(4):
            at = 3 * (4 * pair + to)
            cells = pltpu.roll(near[places[at]], places[at + 1], 1)
            cells = pltpu.roll(cells, places[at + 2], 2)
            both = cells if both is None else jnp.where(group == to, cells, both)
        mask = masks[pair]
        parts = spread([mask * (both[e] - own[pair, e]) for e in range(3)])
        parts = z_apply(to_modes[pair], [fold(part) for part in parts])
        for target in range(16):
            value = None
            for e in range(3):
                at = e * 16 + target
                term = tables[pair, at : at + 1] * parts[e]
                value = term if value is None else value + term
            out[target, pair] = value


def update_kernel(mixed_one, mixed_two, base, gain, out, made, sent):
    copies = []
    for pair in range(PAIRS):
        for chip in range(8):
            lanes = slice(chip * LANES, chip * LANES + LANES)
            tiles = regroup(
                [mixed[2 * chip + core, pair] for core in range(2) for mixed in (mixed_one, mixed_two)]
            )
            for parity in range(2):
                modes = slice(parity * SIDE, parity * SIDE + SIDE)
                for h in range(2):
                    made[pair, h, modes, lanes] = (
                        base[h, pair, modes, lanes]
                        + gain[h, pair, modes, lanes] * tiles[2 * parity + h]
                    )
            if chip % 2 == 1:
                columns = pl.ds((chip - 1) * LANES, 2 * LANES)
                copies.append(
                    pltpu.make_async_copy(
                        made.at[pair, :, :, columns],
                        out.at[:, pair, :, columns],
                        sent.at[pair, chip // 2],
                    )
                )
                copies[-1].start()
    for copy in copies:
        copy.wait()


def smem():
    return pl.BlockSpec(memory_space=pltpu.SMEM)


def vmem():
    return pl.BlockSpec(memory_space=pltpu.VMEM)


def hbm():
    return pl.BlockSpec(memory_space=pltpu.HBM)


def cost(flops, nbytes):
    return pl.CostEstimate(flops=flops, bytes_accessed=nbytes, transcendentals=0)


def shards(modes_now, modes_prev, extents, partner, offset):
    f32 = jnp.float32
    extents = extents.T
    now = modes_now.reshape(2, PAIRS, 2 * SIDE, 1024)
    previous = modes_prev.reshape(2, PAIRS, 2 * SIDE, 1024)
    nbytes = now.size * 4
    wide_shape = jax.ShapeDtypeStruct(now.shape, f32)
    packed_shape = jax.ShapeDtypeStruct((16, PAIRS, SIDE, LANES), f32)
    rows_shape = jax.ShapeDtypeStruct((PAIRS, 3, SIDE, LANES), f32)
    table_shape = jax.ShapeDtypeStruct((PAIRS, 2 * SIDE, LANES), jnp.bfloat16)
    params = pltpu.CompilerParams(vmem_limit_bytes=VMEM_LIMIT)
    wide_scratch = pltpu.VMEM((PAIRS, 2, 2 * SIDE, 1024), f32)
    copied = pltpu.SemaphoreType.DMA((PAIRS,))
    count = lax.axis_size("region")
    upward = [((i + 1) % count, i) for i in range(count)]
    downward = [(i, (i + 1) % count) for i in range(count)]

    encode_scratch = [
        wide_scratch,
        pltpu.VMEM((PAIRS, 16, SIDE, LANES), f32),
        copied,
        copied,
    ]
    encode_params = pltpu.CompilerParams(vmem_limit_bytes=ENCODE_LIMIT)
    with jax.named_scope("encode"):
        sent_two = pl.pallas_call(
            functools.partial(encode_kernel, 1),
            out_shape=packed_shape,
            in_specs=[hbm()],
            out_specs=hbm(),
            scratch_shapes=encode_scratch,
            compiler_params=encode_params,
            cost_estimate=cost(10**6, 2 * nbytes),
        )(now)
    with jax.named_scope("encode_plan"):
        sent_one, y_tables, to_cells, to_modes, masks, places = pl.pallas_call(
            encode_plan_kernel,
            out_shape=(
                packed_shape,
                jax.ShapeDtypeStruct((PAIRS, 48, LANES), f32),
                table_shape,
                table_shape,
                jax.ShapeDtypeStruct((PAIRS, SIDE, LANES), f32),
                jax.ShapeDtypeStruct((36,), jnp.int32),
            ),
            in_specs=[smem(), smem(), smem(), hbm()],
            out_specs=(hbm(), vmem(), vmem(), vmem(), vmem(), smem()),
            scratch_shapes=encode_scratch,
            compiler_params=encode_params,
            cost_estimate=cost(10**6, 2 * nbytes),
        )(extents, partner, offset, lax.optimization_barrier((now, sent_two))[0])

    def rows_of(held):
        with jax.named_scope("rows"):
            return pl.pallas_call(
                rows_kernel,
                out_shape=rows_shape,
                in_specs=[vmem()] * 3,
                out_specs=vmem(),
                compiler_params=params,
                cost_estimate=cost(10**7, nbytes),
            )(y_tables, to_cells, held)

    def force(rows, up, down):
        with jax.named_scope("force"):
            return pl.pallas_call(
                force_kernel,
                out_shape=packed_shape,
                in_specs=[smem()] + [vmem()] * 6,
                out_specs=vmem(),
                scratch_shapes=[pltpu.VMEM((3 * PAIRS, 3, SIDE, LANES), f32)],
                compiler_params=params,
                cost_estimate=cost(10**7, nbytes),
            )(places, y_tables, to_modes, masks, rows, up, down)

    def exchange(blocks):
        return lax.all_to_all(blocks, "line", 0, 0, tiled=True)

    def halo(rows):
        return lax.ppermute(rows, "region", upward), lax.ppermute(rows, "region", downward)

    held_one = exchange(sent_one)
    held_two = exchange(sent_two)
    rows_one = rows_of(held_one)
    up_one, down_one = halo(rows_one)
    with jax.named_scope("free"):
        base, gain = pl.pallas_call(
            free_kernel,
            out_shape=(wide_shape, wide_shape),
            in_specs=[smem(), hbm(), hbm()],
            out_specs=(hbm(), hbm()),
            scratch_shapes=[pltpu.VMEM(now.shape, f32)] * 4 + [pltpu.SemaphoreType.DMA((OWN, 4))],
            compiler_params=pltpu.CompilerParams(vmem_limit_bytes=FREE_LIMIT),
            cost_estimate=cost(10**9, 4 * nbytes),
        )(extents, *lax.optimization_barrier((now, previous, rows_one))[:2])
    down_one, base, gain = lax.optimization_barrier((down_one, base, gain))
    mixed_one = exchange(force(rows_one, up_one, down_one))
    rows_two = rows_of(held_two)
    up_two, down_two = halo(rows_two)
    mixed_two = exchange(force(rows_two, up_two, down_two))
    with jax.named_scope("update"):
        result = pl.pallas_call(
            update_kernel,
            out_shape=wide_shape,
            in_specs=[vmem()] * 4,
            out_specs=hbm(),
            scratch_shapes=[wide_scratch, pltpu.SemaphoreType.DMA((PAIRS, 4))],
            compiler_params=params,
            cost_estimate=cost(10**7, 4 * nbytes),
        )(mixed_one, mixed_two, base, gain)
    return result.reshape(modes_now.shape)


def solution(mesh):
    return jax.shard_map(
        shards,
        mesh=mesh,
        in_specs=(P("region", "line", None), P("region", "line", None), P(), P(), P()),
        out_specs=P("region", "line", None),
        check_vma=False,
    )
```
